128 devices in a mesh: owner: 32 (over x, y, core), dp: 4 (over z).
Axes of the slice: x: 4, y: 4, z: 4, core: 2. Of those that a mesh axis runs over, the one named last changes fastest.
Arguments:
- entity_table: float32 [65536, 400], P('owner'), may hold values from -0.2 to 0.2
- entity_state: float32 [65536], P('owner'), may hold values from 0.002 to 0.02
- phase_table: float32 [7424, 200], replicated, may hold values from -3.1416 to 3.1416
- phase_state: float32 [7424], replicated, may hold values from 1e-05 to 0.0001
- pull_rows: int32 [128, 32, 128], P(('owner', 'dp')), may hold values from 0 to 2047
- head_slot: int32 [128, 512], P(('owner', 'dp')), may hold values from 0 to 4095, as said below
- tail_slot: int32 [128, 512], P(('owner', 'dp')), may hold values from 0 to 4095, as said below
- neg_slot: int32 [128, 2, 1024], P(('owner', 'dp')), may hold values from 0 to 4095, as said below
- relation: int32 [128, 512], P(('owner', 'dp')), may hold values from 0 to 7423
Outputs:
- new_entity: float32 [65536, 400], P('owner')
- new_entity_state: float32 [65536], P('owner')
- new_phase: float32 [7424, 200], replicated
- new_phase_state: float32 [7424], replicated
The draws below stay inside these ranges and needn't reach their ends.
Inputs may be any that keep to these rules, and one draw needn't show every extreme that they name: `head_slot`: slot numbers of the worker's pulled rows, owner-major. `tail_slot`: slot numbers of the worker's pulled rows, owner-major. `neg_slot`: slot numbers of the worker's pulled rows, owner-major.
All inputs are finite; a program needn't handle non-finite values.
Results may differ from the reference program's by a relative error of at most 0.0035.
Values may be sent and summed in bfloat16 or wider, within the bound.
A program may use at most 192 MiB of HBM per device.

```python
import math
import jax
import jax.numpy as jnp
from jax import lax

K = 200
NREL = 7424
GROUP = 256
NEG = 1024
GROUPS = 2
ROWS_OWN = 2048
B_DEV = 512
CAP = 128
WORKERS = 128
ENTS = 65536
N_OWNER = 32


def center_phases(key):
    return jax.random.uniform(jax.random.fold_in(key, 501), (2, K), jnp.float32, -math.pi, math.pi)


def draw_entity_table(key, part):
    centers = center_phases(key)
    key = jax.random.fold_in(key, 21)
    member = jax.random.randint(jax.random.fold_in(key, 1), (ENTS,), 0, 2)
    angles = centers[member]
    amplitude = 0.09
    noise = 0.03 * jax.random.normal(jax.random.fold_in(key, 2), (ENTS, 2 * K), jnp.float32)
    center_part = amplitude * jnp.concatenate([jnp.cos(angles), jnp.sin(angles)], 1)
    return jnp.clip(center_part + noise, -0.2, 0.2).astype(jnp.float32)


def draw_phase_table(key, part):
    centers = center_phases(key)
    key = jax.random.fold_in(key, 22)
    source = jax.random.randint(jax.random.fold_in(key, 1), (NREL,), 0, 2)
    target = jax.random.randint(jax.random.fold_in(key, 2), (NREL,), 0, 2)
    spread = 0.3 * jax.random.normal(jax.random.fold_in(key, 3), (NREL, K), jnp.float32)
    raw = centers[target] - centers[source] + spread
    return jnp.arctan2(jnp.sin(raw), jnp.cos(raw)).astype(jnp.float32)


def hot_owners(key):
    return jax.random.permutation(jax.random.fold_in(key, 77), N_OWNER)


def skewed_slots(key, table, shape):
    first = jax.random.randint(jax.random.fold_in(key, 1), shape, 0, N_OWNER)
    second = jax.random.randint(jax.random.fold_in(key, 2), shape, 0, N_OWNER)
    owner_pick = table[jnp.minimum(first, second)]
    within = jax.random.randint(jax.random.fold_in(key, 3), shape, 0, CAP)
    return (owner_pick * CAP + within).astype(jnp.int32)


def draw_head_slot(key, part):
    table = hot_owners(key)
    key = jax.random.fold_in(key, 11)
    return skewed_slots(key, table, (WORKERS, B_DEV))


def draw_tail_slot(key, part):
    table = hot_owners(key)
    key = jax.random.fold_in(key, 12)
    return skewed_slots(key, table, (WORKERS, B_DEV))


def draw_neg_slot(key, part):
    table = hot_owners(key)
    key = jax.random.fold_in(key, 13)
    return skewed_slots(key, table, (WORKERS, GROUPS, NEG))


def place_ends(entries, rng, low, top_value):
    longest = entries.shape.index(max(entries.shape))
    spots = []
    for shift in (0, 1):
        where = [jax.random.randint(jax.random.fold_in(rng, axis), (), 0, length) for axis, length in enumerate(entries.shape)]
        where[longest] = (where[longest] + shift) % entries.shape[longest]
        spots.append(tuple(where))
    return entries.at[spots[0]].set(low).at[spots[1]].set(top_value)


def block_scale(rng, shape, cuts, smallest, high):
    loudness = 1.0
    for axis_at, blocks in cuts:
        draws = jax.random.uniform(jax.random.fold_in(jax.random.fold_in(rng, 6), axis_at), (blocks,), jnp.float32, smallest / len(cuts), high / len(cuts))
        loudness = loudness * jnp.repeat(jnp.exp(draws), shape[axis_at] // blocks).reshape((-1,) + (1,) * (len(shape) - 1 - axis_at))
    return loudness


def setup_inputs(seed: int = 0) -> dict:
    seeds = jax.random.split(jax.random.key(seed), 10)
    entity_table = draw_entity_table(jax.random.fold_in(seeds[9], 71), 0)
    entity_state = jnp.clip(jnp.exp(math.log(0.02) - 2.30258502 * jax.random.uniform(seeds[1], (ENTS,), jnp.float32) ** block_scale(seeds[1], (ENTS,), ((0, 32),), -0.2, 0.2)), 0.002, 0.02)
    phase_table = draw_phase_table(jax.random.fold_in(seeds[9], 71), 0)
    phase_state = jnp.clip(jnp.exp(jax.random.uniform(seeds[3], (NREL,), jnp.float32, math.log(9.999999747378752e-06), math.log(0.0001))), 9.999999747378752e-06, 0.0001)
    pull_rows = place_ends(jax.random.randint(seeds[4], (WORKERS, N_OWNER, CAP), 0, ROWS_OWN), jax.random.fold_in(seeds[4], 1), 0, ROWS_OWN - 1).astype(jnp.int32)
    head_slot = draw_head_slot(jax.random.fold_in(seeds[9], 71), 0)
    tail_slot = draw_tail_slot(jax.random.fold_in(seeds[9], 71), 0)
    neg_slot = draw_neg_slot(jax.random.fold_in(seeds[9], 71), 0)
    relation = place_ends(jax.random.randint(seeds[8], (WORKERS, B_DEV), 0, NREL), jax.random.fold_in(seeds[8], 1), 0, NREL - 1).astype(jnp.int32)
    return dict(entity_table=entity_table, entity_state=entity_state, phase_table=phase_table, phase_state=phase_state, pull_rows=pull_rows, head_slot=head_slot, tail_slot=tail_slot, neg_slot=neg_slot, relation=relation)


GAMMA = 2.0
RATE = 0.05

def block_grads(heads, tails, negs, phase):
    width = phase.shape[1]
    cosine = jnp.cos(phase)
    sine = jnp.sin(phase)
    head_re = heads[:, :width].astype(jnp.float32)
    head_im = heads[:, width:].astype(jnp.float32)
    rot_re = head_re * cosine - head_im * sine
    rot_im = head_re * sine + head_im * cosine
    rotated = jnp.concatenate([rot_re, rot_im], 1)
    diff = rotated - tails.astype(jnp.float32)
    pos_score = GAMMA - lax.optimization_barrier(jnp.sum(diff * diff, 1))
    rot_half = rotated.astype(jnp.bfloat16)
    rot_wide = rot_half.astype(jnp.float32)
    neg_wide = negs.astype(jnp.float32)
    row_norm = lax.optimization_barrier(jnp.sum(rot_wide * rot_wide, 1))
    neg_norm = lax.optimization_barrier(jnp.sum(neg_wide * neg_wide, 1))
    cross = lax.dot_general(rot_half, negs, (((1,), (1,)), ((), ())), preferred_element_type=jnp.float32)
    neg_score = GAMMA - (row_norm[:, None] + neg_norm[None, :] - 2.0 * cross)
    diff_grad = 2.0 * jax.nn.sigmoid(-pos_score)[:, None] * diff
    neg_weight = jax.nn.sigmoid(neg_score) / negs.shape[0]
    weight_half = neg_weight.astype(jnp.bfloat16)
    rot_grad = diff_grad - 2.0 * lax.optimization_barrier(jnp.sum(neg_weight, 1))[:, None] * rot_wide + 2.0 * jnp.dot(weight_half, negs, preferred_element_type=jnp.float32)
    neg_grad = -2.0 * lax.optimization_barrier(jnp.sum(neg_weight, 0))[:, None] * neg_wide + 2.0 * lax.dot_general(weight_half, rot_half, (((0,), (0,)), ((), ())), preferred_element_type=jnp.float32)
    grad_re = rot_grad[:, :width]
    grad_im = rot_grad[:, width:]
    phase_grad = grad_im * rot_re - grad_re * rot_im
    head_grad = jnp.concatenate([grad_re * cosine + grad_im * sine, grad_im * cosine - grad_re * sine], 1)
    return (head_grad, -diff_grad, neg_grad, phase_grad)

def adagrad(table, state, grad):
    new_state = state + lax.optimization_barrier(jnp.mean(grad * grad, 1))
    return (table - RATE * grad / jnp.sqrt(new_state)[:, None], new_state)

def reference(entity_table, entity_state, phase_table, phase_state, pull_rows, head_slot, tail_slot, neg_slot, relation):
    width_two = entity_table.shape[1]
    bases = (jnp.arange(N_OWNER, dtype=jnp.int32) * ROWS_OWN)[:, None]

    def one_worker(carry, inputs):
        ent_grad, rel_grad = carry
        rows, heads_idx, tails_idx, negs_idx, rel_idx = inputs
        global_rows = (rows + bases).reshape(-1).astype(jnp.int32)
        pulled = entity_table[global_rows].astype(jnp.bfloat16)
        slot_grad = jnp.zeros((global_rows.shape[0], width_two), jnp.float32)
        for block in range(GROUPS):
            hs = heads_idx[block * GROUP:(block + 1) * GROUP]
            ts = tails_idx[block * GROUP:(block + 1) * GROUP]
            ns = negs_idx[block]
            rs = rel_idx[block * GROUP:(block + 1) * GROUP]
            hg, tg, ng, pg = block_grads(pulled[hs], pulled[ts], pulled[ns], phase_table[rs])
            slot_grad = slot_grad.at[hs].add(hg).at[ts].add(tg).at[ns].add(ng)
            rel_grad = rel_grad.at[rs].add(pg)
        ent_grad = ent_grad.at[global_rows].add(slot_grad)
        return ((ent_grad, rel_grad), None)
    start = (jnp.zeros(entity_table.shape, jnp.float32), jnp.zeros(phase_table.shape, jnp.float32))
    (ent_grad, rel_grad), _ = lax.scan(one_worker, start, (pull_rows, head_slot, tail_slot, neg_slot, relation))
    new_entity, new_entity_state = adagrad(entity_table, entity_state, ent_grad)
    new_phase, new_phase_state = adagrad(phase_table, phase_state, rel_grad)
    return (new_entity, new_entity_state, new_phase, new_phase_state)
```

```python
import functools

import jax
import jax.numpy as jnp
from jax import lax
from jax.experimental import pallas as pl
from jax.experimental.pallas import tpu as pltpu
from jax.sharding import PartitionSpec as P

GAMMA = 2.0
RATE = 0.05
LANES = 128
PAIR = 256
BF16 = jnp.bfloat16
F32 = jnp.float32
MESH = pl.DeviceIdType.MESH
VMEM_LIMIT = 60 * 2**20
NT = (((1,), (1,)), ((), ()))
TN = (((0,), (0,)), ((), ()))


def one_hot(rows, base, index):
    at = lax.broadcasted_iota(jnp.int32, (rows, index.shape[1]), 0) + base
    return jnp.where(at == index, 1.0, 0.0).astype(BF16)


def lanes(start, size):
    return pl.ds(pl.multiple_of(start, LANES), size)


def grid_of(owners):
    chips = owners // 2
    along_y = min(4, chips)
    return chips // along_y, along_y


def offset(j, nx, ny):
    dx = j % nx
    return dx, (j // nx + dx) % ny


def partner(me, j, nx, ny, sign):
    chip = me // 2
    dx, dy = offset(j, nx, ny)
    x = (chip // ny + sign * dx + nx) % nx
    y = (chip % ny + sign * dy + ny) % ny
    return (x * ny + y) * 2


def positions(slots, me, nx, ny):
    chip = slots >> 8
    x, y = chip // ny, chip & (ny - 1)
    mine = me // 2
    dx = (mine // ny - x) & (nx - 1)
    dy = (mine % ny - y) & (ny - 1)
    j = ((dy - dx) & (ny - 1)) * nx + dx
    return j * PAIR + (slots & (PAIR - 1))


def as_column(row):
    return jnp.broadcast_to(row, (LANES, row.shape[1])).T[:, :1]


def as_row(column):
    return jnp.broadcast_to(column, (column.shape[0], LANES)).T[:1, :]


def greet(me, owners, dp_me, dps):
    barrier = pltpu.get_barrier_semaphore()

    def hello(k, _):
        pl.semaphore_signal(
            barrier, inc=1, device_id={"owner": (me + k) % owners}, device_id_type=MESH
        )
        return 0

    lax.fori_loop(1, owners, hello, 0)
    for k in range(1, dps):
        pl.semaphore_signal(
            barrier, inc=1, device_id={"dp": (dp_me + k) % dps}, device_id_type=MESH
        )
    pl.semaphore_wait(barrier, owners - 1 + dps - 1)


def block_grads(b, group, neg, used, cosine, sine, grads, phase_grads):
    triples = 2 * group
    cols = lanes(b * group, group)
    tail_cols = lanes(triples + b * group, group)
    neg_cols = lanes(2 * triples + b * neg, neg)
    cos, sin = cosine[:, cols], sine[:, cols]
    width = cos.shape[0]
    heads = used[:, cols].astype(F32)
    head_re, head_im = heads[:width], heads[width:]
    rot_re = head_re * cos - head_im * sin
    rot_im = head_re * sin + head_im * cos
    rotated = jnp.concatenate([rot_re, rot_im], 0)
    diff = rotated - used[:, tail_cols].astype(F32)
    pos_score = GAMMA - jnp.sum(diff * diff, 0, keepdims=True)
    rot_half = rotated.astype(BF16)
    rot_wide = rot_half.astype(F32)
    negs = used[:, neg_cols]
    neg_wide = negs.astype(F32)
    row_norm = as_column(jnp.sum(rot_wide * rot_wide, 0, keepdims=True))
    neg_norm = jnp.sum(neg_wide * neg_wide, 0, keepdims=True)
    cross = lax.dot_general(rot_half, negs, TN, preferred_element_type=F32)
    neg_score = GAMMA - (row_norm + neg_norm - 2.0 * cross)
    weight = jax.nn.sigmoid(neg_score) * (1.0 / neg)
    weight_half = weight.astype(BF16)
    diff_grad = (2.0 * jax.nn.sigmoid(-pos_score)) * diff
    row_sum = as_row(jnp.sum(weight, 1, keepdims=True))
    col_sum = jnp.sum(weight, 0, keepdims=True)
    rot_grad = (
        diff_grad
        - (2.0 * row_sum) * rot_wide
        + 2.0 * lax.dot_general(negs, weight_half, NT, preferred_element_type=F32)
    )
    grads[:, neg_cols] = (
        2.0 * jnp.dot(rot_half, weight_half, preferred_element_type=F32)
        - (2.0 * col_sum) * neg_wide
    ).astype(BF16)
    grads[:, tail_cols] = (-diff_grad).astype(BF16)
    grad_re, grad_im = rot_grad[:width], rot_grad[width:]
    phase_grads[:, cols] = grad_im * rot_re - grad_re * rot_im
    grads[:, cols] = jnp.concatenate(
        [grad_re * cos + grad_im * sin, grad_im * cos - grad_re * sin], 0
    ).astype(BF16)


def pull_kernel(
    owners, group, neg,
    table_hbm, phase_hbm, requests, slots, relation,
    grads, rel_out, asked_out,
    table, phase, table_half, asked, sent, pulled, used, theta, cosine, sine, phase_grads,
    load_sems, ask_send, ask_recv, row_send, row_recv,
):
    nx, ny = grid_of(owners)
    chips = nx * ny
    me = lax.axis_index("owner")
    core = me % 2
    load_table = pltpu.make_async_copy(table_hbm, table, load_sems.at[0])
    load_phase = pltpu.make_async_copy(phase_hbm, phase, load_sems.at[1])
    load_table.start()
    load_phase.start()
    greet(me, owners, 0, 1)

    def ask(j, q):
        to = partner(me, j, nx, ny, -1) + q
        return to, pltpu.make_async_remote_copy(
            src_ref=requests.at[to], dst_ref=asked.at[2 * j + core],
            send_sem=ask_send.at[2 * j + q], recv_sem=ask_recv.at[2 * j + core],
            device_id={"owner": to}, device_id_type=MESH,
        )

    def ask_all(j, _):
        for q in range(2):
            to, copy = ask(j, q)

            @pl.when(to != me)
            def _():
                copy.start()

        return 0

    lax.fori_loop(0, chips, ask_all, 0)
    asked[core] = requests[me]
    load_table.wait()
    table_half[...] = table[...].astype(BF16)

    def row_copy(j, q):
        to = partner(me, j, nx, ny, 1) + q
        return to, pltpu.make_async_remote_copy(
            src_ref=sent.at[2 * j + q],
            dst_ref=pulled.at[:, lanes(j * PAIR + core * LANES, LANES)],
            send_sem=row_send.at[2 * j + q], recv_sem=row_recv.at[2 * j + core],
            device_id={"owner": to}, device_id_type=MESH,
        )

    def wait_from(j, sems, buffer_of):
        for q in range(2):
            @pl.when(partner(me, j, nx, ny, -1) + q != me)
            def _():
                buffer_of(j, q, sems.at[2 * j + q])

    def fetch(j, _):
        for q in range(2):
            @pl.when(partner(me, j, nx, ny, 1) + q != me)
            def _():
                pltpu.make_async_copy(
                    asked.at[2 * j + q], asked.at[2 * j + q], ask_recv.at[2 * j + q]
                ).wait()

        wanted = jnp.concatenate([asked[2 * j], asked[2 * j + 1]], 1)
        rows = jnp.dot(
            table_half[...], one_hot(table_half.shape[1], 0, wanted), preferred_element_type=F32
        ).astype(BF16)
        for q in range(2):
            sent[2 * j + q] = rows[:, q * LANES : (q + 1) * LANES]
            to, copy = row_copy(j, q)

            @pl.when(to != me)
            def _():
                copy.start()

        return 0

    lax.fori_loop(0, chips, fetch, 0)
    pulled[:, lanes(core * LANES, LANES)] = sent[core]

    load_phase.wait()
    rel = relation[...]
    nrel = phase.shape[1]
    width = phase.shape[0]

    def phase_part(start, size):
        part = phase[:, lanes(start, size)]
        high = part.astype(BF16).astype(F32)
        both = jnp.concatenate([high, part - high], 0).astype(BF16)
        return jnp.dot(both, one_hot(size, start, rel), preferred_element_type=F32)

    step = 512
    whole = nrel // step
    theta[...] = jnp.zeros_like(theta)

    def add_phase(k, _):
        theta[...] += phase_part(k * step, step)
        return 0

    lax.fori_loop(0, whole, add_phase, 0)
    if nrel % step:
        theta[...] += phase_part(whole * step, nrel % step)
    angle = theta[:width] + theta[width:]
    cosine[...] = jnp.cos(angle)
    sine[...] = jnp.sin(angle)

    place = positions(slots[...], me, nx, ny)
    uses = slots.shape[1]
    half = chips // 2

    def arrived(j, _):
        for q in range(2):
            @pl.when(partner(me, j, nx, ny, -1) + q != me)
            def _():
                spot = pulled.at[:, lanes(j * PAIR + q * LANES, LANES)]
                pltpu.make_async_copy(spot, spot, row_recv.at[2 * j + q]).wait()

        return 0

    tile = 256
    for part in range(2):
        lax.fori_loop(part * half, (part + 1) * half, arrived, 0)
        base = part * half * PAIR
        for t in range(uses // tile):
            cols = slice(t * tile, (t + 1) * tile)
            found = jnp.dot(
                pulled[:, base : base + half * PAIR],
                one_hot(half * PAIR, base, place[:, cols]),
                preferred_element_type=F32,
            ).astype(BF16)
            used[:, cols] = found if part == 0 else used[:, cols] + found

    for b in range(2):
        block_grads(b, group, neg, used, cosine, sine, grads, phase_grads)

    pushed = phase_grads[...].astype(BF16)

    def rel_part(start, size):
        rel_out[:, lanes(start, size)] = lax.dot_general(
            pushed, one_hot(size, start, rel), NT, preferred_element_type=F32
        ).astype(BF16)

    def add_rel(k, _):
        rel_part(k * step, step)
        return 0

    lax.fori_loop(0, whole, add_rel, 0)
    if nrel % step:
        rel_part(whole * step, nrel % step)

    asked_out[...] = asked[...]

    def sends_done(j, _):
        for q in range(2):
            to, first = ask(j, q)
            _, second = row_copy(j, q)

            @pl.when(to != me)
            def _():
                first.wait_send()

            @pl.when(partner(me, j, nx, ny, 1) + q != me)
            def _():
                second.wait_send()

        return 0

    lax.fori_loop(0, chips, sends_done, 0)


def push_kernel(
    owners, dps,
    grads, slots, asked,
    out,
    sent, received, total, shared, from_dp, full,
    row_send, row_recv, dp_send, dp_recv, all_send, all_recv,
):
    nx, ny = grid_of(owners)
    chips = nx * ny
    me = lax.axis_index("owner")
    dp_me = lax.axis_index("dp")
    core = me % 2
    greet(me, owners, dp_me, dps)
    place = positions(slots[...], me, nx, ny)

    def row_copy(j, q):
        to = partner(me, j, nx, ny, -1) + q
        return to, pltpu.make_async_remote_copy(
            src_ref=sent.at[2 * j + q],
            dst_ref=received.at[:, lanes(j * PAIR + core * LANES, LANES)],
            send_sem=row_send.at[2 * j + q], recv_sem=row_recv.at[2 * j + core],
            device_id={"owner": to}, device_id_type=MESH,
        )

    def push(j, _):
        sums = lax.dot_general(
            grads[...], one_hot(PAIR, j * PAIR, place), NT, preferred_element_type=F32
        ).astype(BF16)
        for q in range(2):
            sent[2 * j + q] = sums[:, q * LANES : (q + 1) * LANES]
            to, copy = row_copy(j, q)

            @pl.when(to != me)
            def _():
                copy.start()

        return 0

    lax.fori_loop(0, chips, push, 0)
    received[:, lanes(core * LANES, LANES)] = sent[core]

    def arrived(j, _):
        for q in range(2):
            @pl.when(partner(me, j, nx, ny, 1) + q != me)
            def _():
                spot = received.at[:, lanes(j * PAIR + q * LANES, LANES)]
                pltpu.make_async_copy(spot, spot, row_recv.at[2 * j + q]).wait()

        return 0

    half = chips // 2
    rows = total.shape[1]
    tile = 256
    for part in range(2):
        lax.fori_loop(part * half, (part + 1) * half, arrived, 0)
        span = slice(part * half * PAIR, (part + 1) * half * PAIR)
        for t in range(rows // tile):
            cols = slice(t * tile, (t + 1) * tile)
            added = lax.dot_general(
                received[:, span], one_hot(tile, t * tile, asked[:, span]), NT,
                preferred_element_type=F32,
            )
            if part == 0:
                total[:, cols] = added
            else:
                total[:, cols] += added

    share = rows // dps
    shared[...] = total[...].astype(BF16)

    def to_dp(k):
        to = (dp_me + k) % dps
        return pltpu.make_async_remote_copy(
            src_ref=shared.at[:, lanes(to * share, share)], dst_ref=from_dp.at[k - 1],
            send_sem=dp_send.at[k - 1], recv_sem=dp_recv.at[k - 1],
            device_id={"dp": to}, device_id_type=MESH,
        )

    mine = lanes(dp_me * share, share)

    def to_all(k):
        to = (dp_me + k) % dps
        return pltpu.make_async_remote_copy(
            src_ref=full.at[:, mine], dst_ref=full.at[:, mine],
            send_sem=all_send.at[k - 1], recv_sem=all_recv.at[k - 1],
            device_id={"dp": to}, device_id_type=MESH,
        )

    for k in range(1, dps):
        to_dp(k).start()
    summed = total[:, mine]
    for k in range(1, dps):
        to_dp(k).wait_recv()
        summed += from_dp[k - 1].astype(F32)
    full[:, mine] = summed.astype(BF16)
    for k in range(1, dps):
        to_all(k).start()
    for k in range(1, dps):
        spot = full.at[:, lanes((dp_me - k + dps) % dps * share, share)]
        pltpu.make_async_copy(spot, spot, all_recv.at[k - 1]).wait()
    out[...] = full[...]
    for k in range(1, dps):
        to_dp(k).wait_send()
        to_all(k).wait_send()

    def sends_done(j, _):
        for q in range(2):
            to, copy = row_copy(j, q)

            @pl.when(to != me)
            def _():
                copy.wait_send()

        return 0

    lax.fori_loop(0, chips, sends_done, 0)


def adagrad_kernel(table, state, grad, new_table, new_state):
    g = grad[...].astype(F32)
    fresh = state[...] + jnp.sum(g * g, 0, keepdims=True) * (1.0 / g.shape[0])
    new_state[...] = fresh
    new_table[...] = table[...] - g * (RATE / jnp.sqrt(fresh))


def adagrad(table, state, grad, tile):
    width, rows = table.shape
    wide = pl.BlockSpec((width, tile), lambda i: (0, i))
    thin = pl.BlockSpec((1, tile), lambda i: (0, i))
    new_table, new_state = pl.pallas_call(
        adagrad_kernel,
        grid=(pl.cdiv(rows, tile),),
        out_shape=(
            jax.ShapeDtypeStruct((width, rows), F32),
            jax.ShapeDtypeStruct((1, rows), F32),
        ),
        in_specs=[wide, thin, wide],
        out_specs=(wide, thin),
        compiler_params=pltpu.CompilerParams(vmem_limit_bytes=VMEM_LIMIT),
    )(table, state[None], grad)
    return new_table.T, new_state[0]


VM = pl.BlockSpec(memory_space=pltpu.VMEM)
HBM = pl.BlockSpec(memory_space=pl.ANY)


def on_device(
    entity_table, entity_state, phase_table, phase_state,
    pull_rows, head_slot, tail_slot, neg_slot, relation,
):
    owners, dps = lax.axis_size("owner"), lax.axis_size("dp")
    table, phase = entity_table.T, phase_table.T
    width, rows = table.shape
    narrow, nrel = phase.shape
    triples = head_slot.shape[1]
    neg = neg_slot.shape[2]
    slots = jnp.concatenate([head_slot, tail_slot, neg_slot.reshape(1, -1)], 1)
    uses = slots.shape[1]
    pulls = owners * LANES
    requests = pull_rows.reshape(owners, 1, LANES)
    dma = pltpu.SemaphoreType.DMA
    grads, rel_grad, asked = pl.pallas_call(
        functools.partial(pull_kernel, owners, triples // 2, neg),
        out_shape=(
            jax.ShapeDtypeStruct((width, uses), BF16),
            jax.ShapeDtypeStruct((narrow, nrel), BF16),
            jax.ShapeDtypeStruct((owners, 1, LANES), jnp.int32),
        ),
        in_specs=[HBM, HBM, VM, VM, VM],
        out_specs=(VM, VM, VM),
        scratch_shapes=[
            pltpu.VMEM((width, rows), F32),
            pltpu.VMEM((narrow, nrel), F32),
            pltpu.VMEM((width, rows), BF16),
            pltpu.VMEM((owners, 1, LANES), jnp.int32),
            pltpu.VMEM((owners, width, LANES), BF16),
            pltpu.VMEM((width, pulls), BF16),
            pltpu.VMEM((width, uses), BF16),
            pltpu.VMEM((width, triples), F32),
            pltpu.VMEM((narrow, triples), F32),
            pltpu.VMEM((narrow, triples), F32),
            pltpu.VMEM((narrow, triples), F32),
            dma((2,)), dma((owners,)), dma((owners,)), dma((owners,)), dma((owners,)),
        ],
        compiler_params=pltpu.CompilerParams(
            collective_id=0, has_side_effects=True, vmem_limit_bytes=VMEM_LIMIT
        ),
        name="pull",
    )(table, phase, requests, slots, relation)
    rel_total = lax.psum(rel_grad, ("owner", "dp"))
    grad = pl.pallas_call(
        functools.partial(push_kernel, owners, dps),
        out_shape=jax.ShapeDtypeStruct((width, rows), BF16),
        in_specs=[VM, VM, VM],
        out_specs=VM,
        scratch_shapes=[
            pltpu.VMEM((owners, width, LANES), BF16),
            pltpu.VMEM((width, pulls), BF16),
            pltpu.VMEM((width, rows), F32),
            pltpu.VMEM((width, rows), BF16),
            pltpu.VMEM((dps - 1, width, rows // dps), BF16),
            pltpu.VMEM((width, rows), BF16),
            dma((owners,)), dma((owners,)),
            dma((dps - 1,)), dma((dps - 1,)), dma((dps - 1,)), dma((dps - 1,)),
        ],
        compiler_params=pltpu.CompilerParams(
            collective_id=1, has_side_effects=True, vmem_limit_bytes=VMEM_LIMIT
        ),
        name="push",
    )(grads, slots, asked.reshape(1, pulls))
    new_entity, new_entity_state = adagrad(table, entity_state, grad, 512)
    new_phase, new_phase_state = adagrad(phase, phase_state, rel_total, 1024)
    return (new_entity, new_entity_state, new_phase, new_phase_state)


def solution(mesh):
    placed = (
        P("owner", None),
        P("owner"),
        P(),
        P(),
        P(("owner", "dp"), None, None),
        P(("owner", "dp"), None),
        P(("owner", "dp"), None),
        P(("owner", "dp"), None, None),
        P(("owner", "dp"), None),
    )
    return jax.shard_map(
        on_device,
        mesh=mesh,
        in_specs=placed,
        out_specs=(P("owner", None), P("owner"), P(), P()),
        check_vma=False,
    )
```

```python
import functools

import jax
import jax.numpy as jnp
from jax import lax
from jax.experimental import pallas as pl
from jax.experimental.pallas import tpu as pltpu
from jax.sharding import PartitionSpec as P

GAMMA = 2.0
RATE = 0.05
LANES = 128
PAIR = 256
BF16 = jnp.bfloat16
F32 = jnp.float32
MESH = pl.DeviceIdType.MESH
VMEM_LIMIT = 60 * 2**20
NT = (((1,), (1,)), ((), ()))
TN = (((0,), (0,)), ((), ()))


def one_hot(rows, base, index):
    at = lax.broadcasted_iota(jnp.int32, (rows, index.shape[1]), 0) + base
    return jnp.where(at == index, 1.0, 0.0).astype(BF16)


def lanes(start, size):
    return pl.ds(pl.multiple_of(start, LANES), size)


def grid_of(owners):
    chips = owners // 2
    along_y = min(4, chips)
    return chips // along_y, along_y


def offset(j, nx, ny):
    dx = j % nx
    return dx, (j // nx + dx) % ny


def partner(me, j, nx, ny, sign):
    chip = me // 2
    dx, dy = offset(j, nx, ny)
    x = (chip // ny + sign * dx + nx) % nx
    y = (chip % ny + sign * dy + ny) % ny
    return (x * ny + y) * 2


def positions(slots, me, nx, ny):
    chip = slots >> 8
    x, y = chip // ny, chip & (ny - 1)
    mine = me // 2
    dx = (mine // ny - x) & (nx - 1)
    dy = (mine % ny - y) & (ny - 1)
    j = ((dy - dx) & (ny - 1)) * nx + dx
    return j * PAIR + (slots & (PAIR - 1))


def as_column(row):
    return jnp.broadcast_to(row, (LANES, row.shape[1])).T[:, :1]


def as_row(column):
    return jnp.broadcast_to(column, (column.shape[0], LANES)).T[:1, :]


def greet(me, owners, dp_me, dps):
    barrier = pltpu.get_barrier_semaphore()

    def hello(k, _):
        pl.semaphore_signal(
            barrier, inc=1, device_id={"owner": (me + k) % owners}, device_id_type=MESH
        )
        return 0

    lax.fori_loop(1, owners, hello, 0)
    for k in range(1, dps):
        pl.semaphore_signal(
            barrier, inc=1, device_id={"dp": (dp_me + k) % dps}, device_id_type=MESH
        )
    pl.semaphore_wait(barrier, owners - 1 + dps - 1)


def block_grads(b, group, neg, used, cosine, sine, grads, phase_grads):
    triples = 2 * group
    cols = lanes(b * group, group)
    tail_cols = lanes(triples + b * group, group)
    neg_cols = lanes(2 * triples + b * neg, neg)
    cos, sin = cosine[:, cols], sine[:, cols]
    width = cos.shape[0]
    heads = used[:, cols].astype(F32)
    head_re, head_im = heads[:width], heads[width:]
    rot_re = head_re * cos - head_im * sin
    rot_im = head_re * sin + head_im * cos
    rotated = jnp.concatenate([rot_re, rot_im], 0)
    diff = rotated - used[:, tail_cols].astype(F32)
    pos_score = GAMMA - jnp.sum(diff * diff, 0, keepdims=True)
    rot_half = rotated.astype(BF16)
    rot_wide = rot_half.astype(F32)
    negs = used[:, neg_cols]
    neg_wide = negs.astype(F32)
    row_norm = as_column(jnp.sum(rot_wide * rot_wide, 0, keepdims=True))
    neg_norm = jnp.sum(neg_wide * neg_wide, 0, keepdims=True)
    cross = lax.dot_general(rot_half, negs, TN, preferred_element_type=F32)
    neg_score = GAMMA - (row_norm + neg_norm - 2.0 * cross)
    weight = jax.nn.sigmoid(neg_score) * (1.0 / neg)
    weight_half = weight.astype(BF16)
    diff_grad = (2.0 * jax.nn.sigmoid(-pos_score)) * diff
    row_sum = as_row(jnp.sum(weight, 1, keepdims=True))
    col_sum = jnp.sum(weight, 0, keepdims=True)
    rot_grad = (
        diff_grad
        - (2.0 * row_sum) * rot_wide
        + 2.0 * lax.dot_general(negs, weight_half, NT, preferred_element_type=F32)
    )
    grads[:, neg_cols] = (
        2.0 * jnp.dot(rot_half, weight_half, preferred_element_type=F32)
        - (2.0 * col_sum) * neg_wide
    ).astype(BF16)
    grads[:, tail_cols] = (-diff_grad).astype(BF16)
    grad_re, grad_im = rot_grad[:width], rot_grad[width:]
    phase_grads[:width, cols] = grad_im * rot_re - grad_re * rot_im
    grads[:, cols] = jnp.concatenate(
        [grad_re * cos + grad_im * sin, grad_im * cos - grad_re * sin], 0
    ).astype(BF16)


def arrive(ref, sem):
    pltpu.make_async_copy(ref, ref, sem).wait()


class RingSum:
    def __init__(self, dp_me, piece, landing, send, recv):
        self.piece, self.landing, self.send, self.recv = piece, landing, send, recv
        self.me, self.right, self.left = dp_me, (dp_me + 1) % 4, (dp_me + 3) % 4
        self.opposite = (dp_me + 2) % 4

    def copy(self, src, slot, to):
        return pltpu.make_async_remote_copy(
            src_ref=src, dst_ref=self.landing[slot],
            send_sem=self.send.at[slot], recv_sem=self.recv.at[slot],
            device_id={"dp": to}, device_id_type=MESH,
        )

    def part(self, slot):
        z, h, to = (
            (self.opposite, 0, self.right),
            (self.opposite, 1, self.left),
            (self.right, 1, self.right),
            (self.left, 0, self.left),
            (self.right, 0, self.right),
            (self.left, 1, self.left),
        )[slot]
        return self.copy(self.piece(z, h), slot, to)

    def begin(self):
        for slot in range(4):
            self.part(slot).start()

    def relay(self):
        for slot, z, h in ((0, self.right, 0), (1, self.left, 1)):
            arrive(self.landing[slot], self.recv.at[slot])
            spot = self.piece(z, h)
            spot[...] = (spot[...].astype(F32) + self.landing[slot][...].astype(F32)).astype(BF16)
            self.part(4 + slot).start()

    def finish(self, h):
        slots = (4, 3) if h == 0 else (5, 2)
        for slot in slots:
            arrive(self.landing[slot], self.recv.at[slot])
        return self.landing[slots[0]][...].astype(F32) + self.landing[slots[1]][...].astype(F32)

    def drain(self):
        for slot in range(6):
            self.part(slot).wait_send()


class RingGather:
    def __init__(self, dp_me, piece, send, recv):
        self.piece, self.send, self.recv = piece, send, recv
        self.me, self.right, self.left = dp_me, (dp_me + 1) % 4, (dp_me + 3) % 4
        self.opposite = (dp_me + 2) % 4

    def part(self, slot):
        z, h, to = (
            (self.me, 0, self.right),
            (self.me, 1, self.left),
            (self.me, 1, self.right),
            (self.me, 0, self.left),
            (self.left, 0, self.right),
            (self.right, 1, self.left),
        )[slot]
        return pltpu.make_async_remote_copy(
            src_ref=self.piece(z, h), dst_ref=self.piece(z, h),
            send_sem=self.send.at[slot], recv_sem=self.recv.at[slot],
            device_id={"dp": to}, device_id_type=MESH,
        )

    def begin(self):
        for slot in range(4):
            self.part(slot).start()

    def relay(self):
        arrive(self.piece(self.left, 0), self.recv.at[0])
        self.part(4).start()
        arrive(self.piece(self.right, 1), self.recv.at[1])
        self.part(5).start()

    def finish(self):
        arrive(self.piece(self.left, 1), self.recv.at[2])
        arrive(self.piece(self.right, 0), self.recv.at[3])
        arrive(self.piece(self.opposite, 0), self.recv.at[4])
        arrive(self.piece(self.opposite, 1), self.recv.at[5])

    def drain(self):
        for slot in range(6):
            self.part(slot).wait_send()


def step_kernel(
    owners, group, neg,
    table_hbm, phase_hbm, requests, slots, relation,
    grad_out, rel_out,
    table, phase, table_half, asked, asked_row, sent, pulled, used, grads,
    theta, cosine, sine, phase_grads,
    received, total, shared, dp_in, full,
    rel, core_in, ring_in, plane_in, rel_sum,
    load_sems, ask_send, ask_recv, row_send, row_recv, back_send, back_recv,
    dp_send, dp_recv, all_send, all_recv,
    core_send, core_recv, ring_send, ring_recv, plane_send, plane_recv,
    spread_send, spread_recv, gather_send, gather_recv,
):
    nx, ny = grid_of(owners)
    chips = nx * ny
    me = lax.axis_index("owner")
    dp_me = lax.axis_index("dp")
    core = me % 2
    load_table = pltpu.make_async_copy(table_hbm, table, load_sems.at[0])
    load_phase = pltpu.make_async_copy(phase_hbm, phase, load_sems.at[1])
    load_table.start()
    load_phase.start()
    greet(me, owners, dp_me, 4)

    def each_core(j, sign, act):
        for q in range(2):
            to = partner(me, j, nx, ny, sign) + q

            @pl.when(to != me)
            def _():
                act(q, to)

    def over_chips(low, high, sign, act):
        def body(j, _):
            each_core(j, sign, functools.partial(act, j))
            return 0

        lax.fori_loop(low, high, body, 0)

    def ask(j, q, to):
        return pltpu.make_async_remote_copy(
            src_ref=requests.at[to], dst_ref=asked.at[2 * j + core],
            send_sem=ask_send.at[2 * j + q], recv_sem=ask_recv.at[2 * j + core],
            device_id={"owner": to}, device_id_type=MESH,
        )

    over_chips(0, chips, -1, lambda j, q, to: ask(j, q, to).start())
    asked[core] = requests[me]
    load_table.wait()
    table_half[...] = table[...].astype(BF16)

    def row_copy(j, q, to):
        return pltpu.make_async_remote_copy(
            src_ref=sent.at[2 * j + q],
            dst_ref=pulled.at[:, lanes(j * PAIR + core * LANES, LANES)],
            send_sem=row_send.at[2 * j + q], recv_sem=row_recv.at[2 * j + core],
            device_id={"owner": to}, device_id_type=MESH,
        )

    def fetch(j, _):
        each_core(j, 1, lambda q, to: arrive(asked.at[2 * j + q], ask_recv.at[2 * j + q]))
        wanted = jnp.concatenate([asked[2 * j], asked[2 * j + 1]], 1)
        asked_row[:, lanes(j * PAIR, PAIR)] = wanted
        rows = jnp.dot(
            table_half[...], one_hot(table_half.shape[1], 0, wanted), preferred_element_type=F32
        ).astype(BF16)
        for q in range(2):
            sent[2 * j + q] = rows[:, q * LANES : (q + 1) * LANES]
        each_core(j, 1, lambda q, to: row_copy(j, q, to).start())
        return 0

    lax.fori_loop(0, chips, fetch, 0)
    pulled[:, lanes(core * LANES, LANES)] = sent[core]

    load_phase.wait()
    rel_index = relation[...]
    nrel = phase.shape[1]
    width = phase.shape[0]
    step = 512
    whole = nrel // step

    def phase_part(start, size):
        part = phase[:, lanes(start, size)]
        high = part.astype(BF16).astype(F32)
        both = jnp.concatenate([high, part - high], 0).astype(BF16)
        return jnp.dot(both, one_hot(size, start, rel_index), preferred_element_type=F32)

    theta[...] = jnp.zeros_like(theta)

    def add_phase(k, _):
        theta[...] += phase_part(k * step, step)
        return 0

    lax.fori_loop(0, whole, add_phase, 0)
    if nrel % step:
        theta[...] += phase_part(whole * step, nrel % step)
    angle = theta[:width] + theta[width:]
    cosine[...] = jnp.cos(angle)
    sine[...] = jnp.sin(angle)

    place = positions(slots[...], me, nx, ny)
    uses = slots.shape[1]
    tile = 256
    cuts = (0, chips // 2, chips - chips // 4, chips)
    for low, high in zip(cuts[:-1], cuts[1:]):
        if low == high:
            continue
        over_chips(
            low, high, -1,
            lambda j, q, to: arrive(
                pulled.at[:, lanes(j * PAIR + q * LANES, LANES)], row_recv.at[2 * j + q]
            ),
        )
        for t in range(uses // tile):
            cols = slice(t * tile, (t + 1) * tile)
            found = jnp.dot(
                pulled[:, low * PAIR : high * PAIR],
                one_hot((high - low) * PAIR, low * PAIR, place[:, cols]),
                preferred_element_type=F32,
            ).astype(BF16)
            used[:, cols] = found if low == 0 else used[:, cols] + found

    phase_grads[width:] = jnp.zeros_like(phase_grads[width:])
    for b in range(2):
        block_grads(b, group, neg, used, cosine, sine, grads, phase_grads)

    pushed = phase_grads[...].astype(BF16)
    per_tile = pushed.shape[0] // 16
    tiles = nrel // LANES

    def rel_part(start_tile, count):
        part = lax.dot_general(
            pushed, one_hot(count * LANES, start_tile * LANES, rel_index), NT,
            preferred_element_type=F32,
        ).astype(BF16)
        for i in range(count):
            rel[pl.ds((start_tile + i) * per_tile, per_tile)] = part[
                :, i * LANES : (i + 1) * LANES
            ].reshape(per_tile, 16, LANES)

    def add_rel(k, _):
        rel_part(k * (step // LANES), step // LANES)
        return 0

    lax.fori_loop(0, whole, add_rel, 0)
    if nrel % step:
        rel_part(whole * (step // LANES), (nrel % step) // LANES)
    units = rel.shape[0]
    if units > tiles * per_tile:
        rel[tiles * per_tile :] = jnp.zeros_like(rel[tiles * per_tile :])

    by_core, by_dp, by_chip = units // 2, units // 8, units // 8 // chips
    core_base = core * by_core
    dp_base = core_base + dp_me * by_dp
    my_base = dp_base + me // 2 * by_chip
    sibling = me + 1 - 2 * core
    swap = pltpu.make_async_remote_copy(
        src_ref=rel.at[pl.ds((1 - core) * by_core, by_core)], dst_ref=core_in,
        send_sem=core_send.at[0], recv_sem=core_recv.at[0],
        device_id={"owner": sibling}, device_id_type=MESH,
    )
    swap.start()
    ring = RingSum(
        dp_me,
        lambda z, h: rel.at[pl.ds(core_base + z * by_dp + h * (by_dp // 2), by_dp // 2)],
        [ring_in.at[i] for i in range(6)], ring_send, ring_recv,
    )

    def plane_copy(j):
        to = partner(me, j, nx, ny, 1) + core
        return pltpu.make_async_remote_copy(
            src_ref=rel.at[pl.ds(dp_base + to // 2 * by_chip, by_chip)], dst_ref=plane_in.at[j],
            send_sem=plane_send.at[j], recv_sem=plane_recv.at[j],
            device_id={"owner": to}, device_id_type=MESH,
        )

    def spread_copy(j):
        to = partner(me, j, nx, ny, 1) + core
        mine = rel_sum.at[pl.ds(my_base, by_chip)]
        return pltpu.make_async_remote_copy(
            src_ref=mine, dst_ref=mine,
            send_sem=spread_send.at[j], recv_sem=spread_recv.at[j],
            device_id={"owner": to}, device_id_type=MESH,
        )

    def loop(low, high, act):
        def body(j, _):
            act(j)
            return 0

        lax.fori_loop(low, high, body, 0)

    rel_ring = RingGather(
        dp_me,
        lambda z, h: rel_sum.at[pl.ds(core_base + z * by_dp + h * (by_dp // 2), by_dp // 2)],
        gather_send, gather_recv,
    )
    share_core = rel_sum.at[pl.ds(core_base, by_core)]
    give = pltpu.make_async_remote_copy(
        src_ref=share_core, dst_ref=share_core,
        send_sem=core_send.at[1], recv_sem=core_recv.at[1],
        device_id={"owner": sibling}, device_id_type=MESH,
    )

    over_chips(0, chips, 1, lambda j, q, to: row_copy(j, q, to).wait_send())

    def back_copy(j, q, to):
        return pltpu.make_async_remote_copy(
            src_ref=sent.at[2 * j + q],
            dst_ref=received.at[:, lanes(j * PAIR + core * LANES, LANES)],
            send_sem=back_send.at[2 * j + q], recv_sem=back_recv.at[2 * j + core],
            device_id={"owner": to}, device_id_type=MESH,
        )

    def push(j, _):
        sums = lax.dot_general(
            grads[...], one_hot(PAIR, j * PAIR, place), NT, preferred_element_type=F32
        ).astype(BF16)
        for q in range(2):
            sent[2 * j + q] = sums[:, q * LANES : (q + 1) * LANES]
        each_core(j, -1, lambda q, to: back_copy(j, q, to).start())
        return 0

    first = min(4, chips)
    later = max(first, chips - 2)
    lax.fori_loop(0, first, push, 0)
    received[:, lanes(core * LANES, LANES)] = sent[core]
    arrive(core_in, core_recv.at[0])
    own_core = rel.at[pl.ds(core_base, by_core)]
    own_core[...] = (own_core[...].astype(F32) + core_in[...].astype(F32)).astype(BF16)
    ring.begin()
    lax.fori_loop(first, later, push, 0)
    ring.relay()
    lax.fori_loop(later, chips, push, 0)
    for h in range(2):
        spot = ring.piece(dp_me, h)
        spot[...] = (spot[...].astype(F32) + ring.finish(h)).astype(BF16)
    loop(1, chips, lambda j: plane_copy(j).start())

    half = chips // 2 if chips > 1 else chips
    rows = total.shape[1]

    def scatter(low, high):
        over_chips(
            low, high, 1,
            lambda j, q, to: arrive(
                received.at[:, lanes(j * PAIR + q * LANES, LANES)], back_recv.at[2 * j + q]
            ),
        )
        span = slice(low * PAIR, high * PAIR)
        for t in range(rows // tile):
            cols = slice(t * tile, (t + 1) * tile)
            added = lax.dot_general(
                received[:, span], one_hot(tile, t * tile, asked_row[:, span]), NT,
                preferred_element_type=F32,
            )
            if low == 0:
                total[:, cols] = added
            else:
                total[:, cols] += added

    scatter(0, half)
    mine = rel.at[pl.ds(my_base, by_chip)][...].astype(F32)

    def add_plane(j, value):
        arrive(plane_in.at[j], plane_recv.at[j])
        return value + plane_in[j].astype(F32)

    rel_sum[pl.ds(my_base, by_chip)] = lax.fori_loop(1, chips, add_plane, mine).astype(BF16)
    loop(1, chips, lambda j: spread_copy(j).start())

    def spread_in(j):
        chip = partner(me, j, nx, ny, -1) // 2
        arrive(rel_sum.at[pl.ds(dp_base + chip * by_chip, by_chip)], spread_recv.at[j])

    loop(1, chips, spread_in)
    rel_ring.begin()
    if half < chips:
        scatter(half, chips)

    share = rows // 4
    split = total.shape[0] // 32 * 16
    shared[...] = total[...].astype(BF16)

    def piece_of(ref):
        def piece(z, h):
            features = pl.ds(0, split) if h == 0 else pl.ds(split, ref.shape[0] - split)
            return ref.at[features, lanes(z * share, share)]

        return piece

    big = shared.shape[0] - split
    dp_ring = RingSum(
        dp_me, piece_of(shared),
        [dp_in.at[i, pl.ds(0, big if i in (1, 2, 5) else split)] for i in range(6)],
        dp_send, dp_recv,
    )
    dp_ring.begin()
    rel_ring.relay()
    dp_ring.relay()
    rel_ring.finish()
    give.start()
    all_ring = RingGather(dp_me, piece_of(full), all_send, all_recv)
    for h in range(2):
        own = total.at[pl.ds(0, split) if h == 0 else pl.ds(split, big), lanes(dp_me * share, share)]
        all_ring.piece(dp_me, h)[...] = (own[...] + dp_ring.finish(h)).astype(BF16)
    all_ring.begin()
    arrive(rel_sum.at[pl.ds((1 - core) * by_core, by_core)], core_recv.at[1])

    def lay(t):
        rel_out[:, lanes(t * LANES, LANES)] = rel_sum[pl.ds(t * per_tile, per_tile)].reshape(
            per_tile * 16, LANES
        )

    loop(0, tiles, lay)
    all_ring.relay()
    swap.wait_send()
    give.wait_send()
    ring.drain()
    rel_ring.drain()
    dp_ring.drain()
    loop(1, chips, lambda j: plane_copy(j).wait_send())
    loop(1, chips, lambda j: spread_copy(j).wait_send())
    over_chips(0, chips, -1, lambda j, q, to: ask(j, q, to).wait_send())
    over_chips(0, chips, -1, lambda j, q, to: back_copy(j, q, to).wait_send())
    all_ring.finish()
    grad_out[...] = full[...]
    all_ring.drain()


def adagrad_kernel(table, state, grad, new_table, new_state):
    g = grad[: table.shape[0]].astype(F32)
    fresh = state[...] + jnp.sum(g * g, 0, keepdims=True) * (1.0 / g.shape[0])
    new_state[...] = fresh
    new_table[...] = table[...] - g * (RATE / jnp.sqrt(fresh))


def adagrad(table, state, grad, tile):
    width, rows = table.shape
    wide = pl.BlockSpec((width, tile), lambda i: (0, i))
    thin = pl.BlockSpec((1, tile), lambda i: (0, i))
    new_table, new_state = pl.pallas_call(
        adagrad_kernel,
        grid=(pl.cdiv(rows, tile),),
        out_shape=(
            jax.ShapeDtypeStruct((width, rows), F32),
            jax.ShapeDtypeStruct((1, rows), F32),
        ),
        in_specs=[wide, thin, pl.BlockSpec((grad.shape[0], tile), lambda i: (0, i))],
        out_specs=(wide, thin),
        compiler_params=pltpu.CompilerParams(vmem_limit_bytes=VMEM_LIMIT),
    )(table, state[None], grad)
    return new_table.T, new_state.reshape(rows)


VM = pl.BlockSpec(memory_space=pltpu.VMEM)
HBM = pl.BlockSpec(memory_space=pl.ANY)


def on_device(
    entity_table, entity_state, phase_table, phase_state,
    pull_rows, head_slot, tail_slot, neg_slot, relation,
):
    owners, dps = lax.axis_size("owner"), lax.axis_size("dp")
    table, phase = entity_table.T, phase_table.T
    width, rows = table.shape
    narrow, nrel = phase.shape
    triples = head_slot.shape[1]
    neg = neg_slot.shape[2]
    slots = jnp.concatenate([head_slot, tail_slot, neg_slot.reshape(1, -1)], 1)
    uses = slots.shape[1]
    pulls = owners * LANES
    requests = pull_rows.reshape(owners, 1, LANES)
    dma = pltpu.SemaphoreType.DMA
    chips = owners // 2
    padded = -(-narrow // 16) * 16
    units = -(-nrel // LANES * padded // 16 // (16 * chips)) * 16 * chips
    big = width - width // 32 * 16
    grad, rel_total = pl.pallas_call(
        functools.partial(step_kernel, owners, triples // 2, neg),
        out_shape=(
            jax.ShapeDtypeStruct((width, rows), BF16),
            jax.ShapeDtypeStruct((padded, nrel), BF16),
        ),
        in_specs=[HBM, HBM, VM, VM, VM],
        out_specs=(VM, VM),
        scratch_shapes=[
            pltpu.VMEM((width, rows), F32),
            pltpu.VMEM((narrow, nrel), F32),
            pltpu.VMEM((width, rows), BF16),
            pltpu.VMEM((owners, 1, LANES), jnp.int32),
            pltpu.VMEM((1, pulls), jnp.int32),
            pltpu.VMEM((owners, width, LANES), BF16),
            pltpu.VMEM((width, pulls), BF16),
            pltpu.VMEM((width, uses), BF16),
            pltpu.VMEM((width, uses), BF16),
            pltpu.VMEM((width, triples), F32),
            pltpu.VMEM((narrow, triples), F32),
            pltpu.VMEM((narrow, triples), F32),
            pltpu.VMEM((padded, triples), F32),
            pltpu.VMEM((width, pulls), BF16),
            pltpu.VMEM((width, rows), F32),
            pltpu.VMEM((width, rows), BF16),
            pltpu.VMEM((6, big, rows // 4), BF16),
            pltpu.VMEM((width, rows), BF16),
            pltpu.VMEM((units, 16, LANES), BF16),
            pltpu.VMEM((units // 2, 16, LANES), BF16),
            pltpu.VMEM((6, units // 16, 16, LANES), BF16),
            pltpu.VMEM((chips, units // 8 // chips, 16, LANES), BF16),
            pltpu.VMEM((units, 16, LANES), BF16),
            dma((2,)),
            dma((owners,)), dma((owners,)), dma((owners,)), dma((owners,)),
            dma((owners,)), dma((owners,)),
            dma((6,)), dma((6,)), dma((6,)), dma((6,)),
            dma((2,)), dma((2,)), dma((6,)), dma((6,)), dma((chips,)), dma((chips,)),
            dma((chips,)), dma((chips,)), dma((6,)), dma((6,)),
        ],
        compiler_params=pltpu.CompilerParams(
            collective_id=0, has_side_effects=True, vmem_limit_bytes=VMEM_LIMIT
        ),
        name="step",
    )(table, phase, requests, slots, relation)
    new_entity, new_entity_state = adagrad(table, entity_state, grad, 512)
    new_phase, new_phase_state = adagrad(phase, phase_state, rel_total, 1024)
    return (new_entity, new_entity_state, new_phase, new_phase_state)


def solution(mesh):
    placed = (
        P("owner", None),
        P("owner"),
        P(),
        P(),
        P(("owner", "dp"), None, None),
        P(("owner", "dp"), None),
        P(("owner", "dp"), None),
        P(("owner", "dp"), None, None),
        P(("owner", "dp"), None),
    )
    return jax.shard_map(
        on_device,
        mesh=mesh,
        in_specs=placed,
        out_specs=(P("owner", None), P("owner"), P(), P()),
        check_vma=False,
    )
```

```python
import functools

import jax
import jax.numpy as jnp
from jax import lax
from jax.experimental import pallas as pl
from jax.experimental.pallas import tpu as pltpu
from jax.sharding import PartitionSpec as P

GAMMA = 2.0
RATE = 0.05
LANES = 128
PAIR = 256
BF16 = jnp.bfloat16
F32 = jnp.float32
MESH = pl.DeviceIdType.MESH
VMEM_LIMIT = 60 * 2**20
NT = (((1,), (1,)), ((), ()))
TN = (((0,), (0,)), ((), ()))


def one_hot(rows, base, index):
    at = lax.broadcasted_iota(jnp.int32, (rows, index.shape[1]), 0) + base
    return jnp.where(at == index, 1.0, 0.0).astype(BF16)


def lanes(start, size):
    return pl.ds(pl.multiple_of(start, LANES), size)


def grid_of(owners):
    chips = owners // 2
    along_y = min(4, chips)
    return chips // along_y, along_y


def offset(j, nx, ny):
    dx = j % nx
    return dx, (j // nx + dx) % ny


def partner(me, j, nx, ny, sign):
    chip = me // 2
    dx, dy = offset(j, nx, ny)
    x = (chip // ny + sign * dx + nx) % nx
    y = (chip % ny + sign * dy + ny) % ny
    return (x * ny + y) * 2


def positions(slots, me, nx, ny):
    chip = slots >> 8
    way = 1 - 2 * ((slots >> 7) & 1)
    x, y = chip // ny, chip & (ny - 1)
    mine = me // 2
    dx = (way * (mine // ny - x)) & (nx - 1)
    dy = (way * (mine % ny - y)) & (ny - 1)
    j = ((dy - dx) & (ny - 1)) * nx + dx
    return j * PAIR + (slots & (PAIR - 1))


def as_column(row):
    return jnp.broadcast_to(row, (LANES, row.shape[1])).T[:, :1]


def as_row(column):
    return jnp.broadcast_to(column, (column.shape[0], LANES)).T[:1, :]


def greet(me, owners, dp_me, dps):
    barrier = pltpu.get_barrier_semaphore()

    def hello(k, _):
        pl.semaphore_signal(
            barrier, inc=1, device_id={"owner": (me + k) % owners}, device_id_type=MESH
        )
        return 0

    lax.fori_loop(1, owners, hello, 0)
    for k in range(1, dps):
        pl.semaphore_signal(
            barrier, inc=1, device_id={"dp": (dp_me + k) % dps}, device_id_type=MESH
        )
    pl.semaphore_wait(barrier, owners - 1 + dps - 1)


def block_grads(b, group, neg, used, cosine, sine, grads, phase_grads):
    triples = 2 * group
    cols = lanes(b * group, group)
    tail_cols = lanes(triples + b * group, group)
    neg_cols = lanes(2 * triples + b * neg, neg)
    cos, sin = cosine[:, cols], sine[:, cols]
    width = cos.shape[0]
    heads = used[:, cols].astype(F32)
    head_re, head_im = heads[:width], heads[width:]
    rot_re = head_re * cos - head_im * sin
    rot_im = head_re * sin + head_im * cos
    rotated = jnp.concatenate([rot_re, rot_im], 0)
    diff = rotated - used[:, tail_cols].astype(F32)
    pos_score = GAMMA - jnp.sum(diff * diff, 0, keepdims=True)
    rot_half = rotated.astype(BF16)
    rot_wide = rot_half.astype(F32)
    negs = used[:, neg_cols]
    neg_wide = negs.astype(F32)
    row_norm = as_column(jnp.sum(rot_wide * rot_wide, 0, keepdims=True))
    neg_norm = jnp.sum(neg_wide * neg_wide, 0, keepdims=True)
    cross = lax.dot_general(rot_half, negs, TN, preferred_element_type=F32)
    neg_score = GAMMA - (row_norm + neg_norm - 2.0 * cross)
    weight = jax.nn.sigmoid(neg_score) * (1.0 / neg)
    weight_half = weight.astype(BF16)
    diff_grad = (2.0 * jax.nn.sigmoid(-pos_score)) * diff
    row_sum = as_row(jnp.sum(weight, 1, keepdims=True))
    col_sum = jnp.sum(weight, 0, keepdims=True)
    rot_grad = (
        diff_grad
        - (2.0 * row_sum) * rot_wide
        + 2.0 * lax.dot_general(negs, weight_half, NT, preferred_element_type=F32)
    )
    grads[:, neg_cols] = (
        2.0 * jnp.dot(rot_half, weight_half, preferred_element_type=F32)
        - (2.0 * col_sum) * neg_wide
    ).astype(BF16)
    grads[:, tail_cols] = (-diff_grad).astype(BF16)
    grad_re, grad_im = rot_grad[:width], rot_grad[width:]
    phase_grads[:width, cols] = grad_im * rot_re - grad_re * rot_im
    grads[:, cols] = jnp.concatenate(
        [grad_re * cos + grad_im * sin, grad_im * cos - grad_re * sin], 0
    ).astype(BF16)


def arrive(ref, sem):
    pltpu.make_async_copy(ref, ref, sem).wait()


class RingSum:
    def __init__(self, dp_me, piece, landing, send, recv):
        self.piece, self.landing, self.send, self.recv = piece, landing, send, recv
        self.me, self.right, self.left = dp_me, (dp_me + 1) % 4, (dp_me + 3) % 4
        self.opposite = (dp_me + 2) % 4

    def copy(self, src, slot, to):
        return pltpu.make_async_remote_copy(
            src_ref=src, dst_ref=self.landing[slot],
            send_sem=self.send.at[slot], recv_sem=self.recv.at[slot],
            device_id={"dp": to}, device_id_type=MESH,
        )

    def part(self, slot):
        z, h, to = (
            (self.opposite, 0, self.right),
            (self.opposite, 1, self.left),
            (self.right, 1, self.right),
            (self.left, 0, self.left),
            (self.right, 0, self.right),
            (self.left, 1, self.left),
        )[slot]
        return self.copy(self.piece(z, h), slot, to)

    def begin(self):
        for slot in range(4):
            self.part(slot).start()

    def relay(self):
        for slot, z, h in ((0, self.right, 0), (1, self.left, 1)):
            arrive(self.landing[slot], self.recv.at[slot])
            spot = self.piece(z, h)
            spot[...] = (spot[...].astype(F32) + self.landing[slot][...].astype(F32)).astype(BF16)
            self.part(4 + slot).start()

    def finish(self, h):
        slots = (4, 3) if h == 0 else (5, 2)
        for slot in slots:
            arrive(self.landing[slot], self.recv.at[slot])
        return self.landing[slots[0]][...].astype(F32) + self.landing[slots[1]][...].astype(F32)

    def drain(self):
        for slot in range(6):
            self.part(slot).wait_send()


class RingGather:
    def __init__(self, dp_me, piece, send, recv):
        self.piece, self.send, self.recv = piece, send, recv
        self.me, self.right, self.left = dp_me, (dp_me + 1) % 4, (dp_me + 3) % 4
        self.opposite = (dp_me + 2) % 4

    def part(self, slot):
        z, h, to = (
            (self.me, 0, self.right),
            (self.me, 1, self.left),
            (self.me, 1, self.right),
            (self.me, 0, self.left),
            (self.left, 0, self.right),
            (self.right, 1, self.left),
        )[slot]
        return pltpu.make_async_remote_copy(
            src_ref=self.piece(z, h), dst_ref=self.piece(z, h),
            send_sem=self.send.at[slot], recv_sem=self.recv.at[slot],
            device_id={"dp": to}, device_id_type=MESH,
        )

    def begin(self):
        for slot in range(4):
            self.part(slot).start()

    def relay(self):
        arrive(self.piece(self.left, 0), self.recv.at[0])
        self.part(4).start()
        arrive(self.piece(self.right, 1), self.recv.at[1])
        self.part(5).start()

    def finish(self):
        arrive(self.piece(self.left, 1), self.recv.at[2])
        arrive(self.piece(self.right, 0), self.recv.at[3])
        arrive(self.piece(self.opposite, 0), self.recv.at[4])
        arrive(self.piece(self.opposite, 1), self.recv.at[5])

    def drain(self):
        for slot in range(6):
            self.part(slot).wait_send()


def step_kernel(
    owners, group, neg,
    table_hbm, phase_hbm, requests, slots, relation,
    grad_out, rel_out,
    table, phase, table_half, asked, asked_row, sent, pulled, used, grads,
    theta, cosine, sine, phase_grads,
    received, total, shared, dp_in, full,
    rel, core_in, halved, ring_in, plane_in, rel_sum,
    load_sems, ask_send, ask_recv, row_send, row_recv, back_send, back_recv,
    dp_send, dp_recv, all_send, all_recv,
    core_send, core_recv, ring_send, ring_recv, plane_send, plane_recv,
    spread_send, spread_recv, gather_send, gather_recv,
):
    nx, ny = grid_of(owners)
    chips = nx * ny
    me = lax.axis_index("owner")
    dp_me = lax.axis_index("dp")
    core = me % 2
    load_table = pltpu.make_async_copy(table_hbm, table, load_sems.at[0])
    load_phase = pltpu.make_async_copy(phase_hbm, phase, load_sems.at[1])
    load_table.start()
    load_phase.start()
    greet(me, owners, dp_me, 4)

    def owner_at(j, q):
        return partner(me, j, nx, ny, 2 * q - 1) + q

    def worker_at(j, q):
        return partner(me, j, nx, ny, 1 - 2 * core) + q

    def each_core(j, place_of, act):
        for q in range(2):
            to = place_of(j, q)

            @pl.when(to != me)
            def _():
                act(q, to)

    def over_chips(low, high, place_of, act):
        def body(j, _):
            each_core(j, place_of, functools.partial(act, j))
            return 0

        lax.fori_loop(low, high, body, 0)

    def loop(low, high, act):
        def body(j, _):
            act(j)
            return 0

        lax.fori_loop(low, high, body, 0)

    def ask(j, q, to):
        return pltpu.make_async_remote_copy(
            src_ref=requests.at[to], dst_ref=asked.at[2 * j + core],
            send_sem=ask_send.at[2 * j + q], recv_sem=ask_recv.at[2 * j + core],
            device_id={"owner": to}, device_id_type=MESH,
        )

    over_chips(0, chips, owner_at, lambda j, q, to: ask(j, q, to).start())
    asked[core] = requests[me]
    load_table.wait()
    table_half[...] = table[...].astype(BF16)

    def row_copy(j, q, to):
        return pltpu.make_async_remote_copy(
            src_ref=sent.at[2 * j + q],
            dst_ref=pulled.at[:, lanes(j * PAIR + core * LANES, LANES)],
            send_sem=row_send.at[2 * j + q], recv_sem=row_recv.at[2 * j + core],
            device_id={"owner": to}, device_id_type=MESH,
        )

    def fetch(j, _):
        each_core(j, worker_at, lambda q, to: arrive(asked.at[2 * j + q], ask_recv.at[2 * j + q]))
        wanted = jnp.concatenate([asked[2 * j], asked[2 * j + 1]], 1)
        asked_row[:, lanes(j * PAIR, PAIR)] = wanted
        rows = jnp.dot(
            table_half[...], one_hot(table_half.shape[1], 0, wanted), preferred_element_type=F32
        ).astype(BF16)
        for q in range(2):
            sent[2 * j + q] = rows[:, q * LANES : (q + 1) * LANES]
        each_core(j, worker_at, lambda q, to: row_copy(j, q, to).start())
        return 0

    lax.fori_loop(0, chips, fetch, 0)
    pulled[:, lanes(core * LANES, LANES)] = sent[core]

    load_phase.wait()
    rel_index = relation[...]
    nrel = phase.shape[1]
    width = phase.shape[0]
    step = 1024
    whole = nrel // step

    def phase_part(start, size):
        part = phase[:, lanes(start, size)]
        high = part.astype(BF16).astype(F32)
        both = jnp.concatenate([high, part - high], 0).astype(BF16)
        return jnp.dot(both, one_hot(size, start, rel_index), preferred_element_type=F32)

    theta[...] = jnp.zeros_like(theta)

    def add_phase(k, _):
        theta[...] += phase_part(k * step, step)
        return 0

    lax.fori_loop(0, whole, add_phase, 0)
    if nrel % step:
        theta[...] += phase_part(whole * step, nrel % step)
    angle = theta[:width] + theta[width:]
    cosine[...] = jnp.cos(angle)
    sine[...] = jnp.sin(angle)

    place = positions(slots[...], me, nx, ny)
    uses = slots.shape[1]
    tile = 256
    cuts = (0, chips // 2, chips - chips // 4, chips)
    for low, high in zip(cuts[:-1], cuts[1:]):
        if low == high:
            continue
        over_chips(
            low, high, owner_at,
            lambda j, q, to: arrive(
                pulled.at[:, lanes(j * PAIR + q * LANES, LANES)], row_recv.at[2 * j + q]
            ),
        )
        for t in range(uses // tile):
            cols = slice(t * tile, (t + 1) * tile)
            found = jnp.dot(
                pulled[:, low * PAIR : high * PAIR],
                one_hot((high - low) * PAIR, low * PAIR, place[:, cols]),
                preferred_element_type=F32,
            ).astype(BF16)
            used[:, cols] = found if low == 0 else used[:, cols] + found

    phase_grads[width:] = jnp.zeros_like(phase_grads[width:])
    for b in range(2):
        block_grads(b, group, neg, used, cosine, sine, grads, phase_grads)

    pushed = phase_grads[...].astype(BF16)
    per_tile = pushed.shape[0] // 16
    tiles = nrel // LANES

    def rel_part(start_tile, count):
        part = lax.dot_general(
            pushed, one_hot(count * LANES, start_tile * LANES, rel_index), NT,
            preferred_element_type=F32,
        ).astype(BF16)
        for i in range(count):
            rel[pl.ds((start_tile + i) * per_tile, per_tile)] = part[
                :, i * LANES : (i + 1) * LANES
            ].reshape(per_tile, 16, LANES)

    def add_rel(k, _):
        rel_part(k * (step // LANES), step // LANES)
        return 0

    lax.fori_loop(0, whole, add_rel, 0)
    if nrel % step:
        rel_part(whole * (step // LANES), (nrel % step) // LANES)
    units = rel.shape[0]
    if units > tiles * per_tile:
        rel[tiles * per_tile :] = jnp.zeros_like(rel[tiles * per_tile :])

    by_chip, by_piece = units // 2 // chips, units // 8 // chips
    by_core = units // 2
    my_chip = me // 2
    sibling = me + 1 - 2 * core
    my_chip_base = core * by_core + my_chip * by_chip
    my_piece = rel_sum.at[pl.ds(my_chip_base + dp_me * by_piece, by_piece)]
    swap = pltpu.make_async_remote_copy(
        src_ref=rel.at[pl.ds((1 - core) * by_core, by_core)], dst_ref=core_in,
        send_sem=core_send.at[0], recv_sem=core_recv.at[0],
        device_id={"owner": sibling}, device_id_type=MESH,
    )
    swap.start()
    some = chips // 2
    ring = RingSum(
        dp_me, lambda z, h: halved.at[pl.ds(h * some, some), z],
        [ring_in.at[i] for i in range(6)], ring_send, ring_recv,
    )

    def plane_peer(j, sign):
        return partner(me, j, nx, ny, sign * (1 - 2 * core)) + core

    def plane_copy(j):
        to = plane_peer(j, 1)
        return pltpu.make_async_remote_copy(
            src_ref=halved.at[to // 2, dp_me], dst_ref=plane_in.at[j],
            send_sem=plane_send.at[j], recv_sem=plane_recv.at[j],
            device_id={"owner": to}, device_id_type=MESH,
        )

    def along_dp(k):
        return pltpu.make_async_remote_copy(
            src_ref=my_piece, dst_ref=my_piece,
            send_sem=gather_send.at[k - 1], recv_sem=gather_recv.at[k - 1],
            device_id={"dp": (dp_me + k) % 4}, device_id_type=MESH,
        )

    def spread_copy(j):
        mine = rel_sum.at[pl.ds(my_chip_base, by_chip)]
        return pltpu.make_async_remote_copy(
            src_ref=mine, dst_ref=mine,
            send_sem=spread_send.at[j], recv_sem=spread_recv.at[j],
            device_id={"owner": plane_peer(j, 1)}, device_id_type=MESH,
        )

    share_core = rel_sum.at[pl.ds(core * by_core, by_core)]
    give = pltpu.make_async_remote_copy(
        src_ref=share_core, dst_ref=share_core,
        send_sem=core_send.at[1], recv_sem=core_recv.at[1],
        device_id={"owner": sibling}, device_id_type=MESH,
    )

    over_chips(0, chips, worker_at, lambda j, q, to: row_copy(j, q, to).wait_send())
    features = total.shape[0]
    middle = -(-features // 32) * 16
    parts = ((0, middle), (middle, features))

    def back_copy(part, j, q, to):
        low, high = parts[part]
        return pltpu.make_async_remote_copy(
            src_ref=sent.at[2 * j + q, pl.ds(low, high - low)],
            dst_ref=received.at[pl.ds(low, high - low), lanes(j * PAIR + core * LANES, LANES)],
            send_sem=back_send.at[part, 2 * j + q], recv_sem=back_recv.at[part, 2 * j + core],
            device_id={"owner": to}, device_id_type=MESH,
        )

    def push(j, _):
        sums = lax.dot_general(
            grads[...], one_hot(PAIR, j * PAIR, place), NT, preferred_element_type=F32
        ).astype(BF16)
        for q in range(2):
            sent[2 * j + q] = sums[:, q * LANES : (q + 1) * LANES]
        each_core(j, owner_at, lambda q, to: back_copy(0, j, q, to).start())
        return 0

    first = min(4, chips)
    later = max(first, chips - 3)
    lax.fori_loop(0, first, push, 0)
    received[:, lanes(core * LANES, LANES)] = sent[core]
    arrive(core_in, core_recv.at[0])

    def add_core(p):
        own = rel[pl.ds(core * by_core + p * by_chip, by_chip)].astype(F32)
        both = own + core_in[pl.ds(p * by_chip, by_chip)].astype(F32)
        halved[p] = both.astype(BF16).reshape(4, by_piece, 16, LANES)

    loop(0, chips, add_core)
    ring.begin()
    lax.fori_loop(first, later, push, 0)
    ring.relay()
    lax.fori_loop(later, chips, push, 0)
    over_chips(0, chips, owner_at, lambda j, q, to: back_copy(1, j, q, to).start())
    for h in range(2):
        spot = ring.piece(dp_me, h)
        spot[...] = (spot[...].astype(F32) + ring.finish(h)).astype(BF16)
    loop(1, chips, lambda j: plane_copy(j).start())

    rows = total.shape[1]
    share = rows // 4

    def scatter(part):
        low, high = parts[part]
        over_chips(
            0, chips, worker_at,
            lambda j, q, to: arrive(
                received.at[pl.ds(low, high - low), lanes(j * PAIR + q * LANES, LANES)],
                back_recv.at[part, 2 * j + q],
            ),
        )
        for t in range(rows // tile):
            cols = slice(t * tile, (t + 1) * tile)
            added = lax.dot_general(
                received[low:high], one_hot(tile, t * tile, asked_row[...]), NT,
                preferred_element_type=F32,
            )
            total[low:high, cols] = added
            shared[low:high, cols] = added.astype(BF16)

    def halves(part):
        low, high = parts[part]
        cut = low + -(-(high - low) // 32) * 16
        return ((low, cut - low), (cut, high - cut))

    def piece_of(ref, part):
        return lambda z, h: ref.at[pl.ds(*halves(part)[h]), lanes(z * share, share)]

    def dp_sum(part):
        sizes = [halves(part)[h][1] for h in (0, 1, 1, 0, 0, 1)]
        return RingSum(
            dp_me, piece_of(shared, part),
            [dp_in.at[part, i, pl.ds(0, sizes[i])] for i in range(6)],
            dp_send.at[part], dp_recv.at[part],
        )

    sums = [dp_sum(part) for part in range(2)]
    alls = [
        RingGather(dp_me, piece_of(full, part), all_send.at[part], all_recv.at[part])
        for part in range(2)
    ]

    def settle(part):
        for h in range(2):
            own = piece_of(total, part)(dp_me, h)
            alls[part].piece(dp_me, h)[...] = (own[...] + sums[part].finish(h)).astype(BF16)
        alls[part].begin()

    scatter(0)
    sums[0].begin()

    def add_plane(j, value):
        arrive(plane_in.at[j], plane_recv.at[j])
        return value + plane_in[j].astype(F32)

    my_piece[...] = lax.fori_loop(
        1, chips, add_plane, halved[my_chip, dp_me].astype(F32)
    ).astype(BF16)
    for k in range(1, 4):
        along_dp(k).start()
    sums[0].relay()
    scatter(1)
    sums[1].begin()
    for k in range(1, 4):
        z = (dp_me - k + 4) % 4
        arrive(
            rel_sum.at[pl.ds(my_chip_base + z * by_piece, by_piece)], gather_recv.at[k - 1]
        )
    loop(1, chips, lambda j: spread_copy(j).start())
    settle(0)
    sums[1].relay()
    alls[0].relay()
    settle(1)
    alls[1].relay()

    def spread_in(j):
        chip = plane_peer(j, -1) // 2
        arrive(rel_sum.at[pl.ds(core * by_core + chip * by_chip, by_chip)], spread_recv.at[j])

    loop(1, chips, spread_in)
    give.start()
    swap.wait_send()
    ring.drain()
    for part in range(2):
        sums[part].drain()
    for k in range(1, 4):
        along_dp(k).wait_send()
    loop(1, chips, lambda j: plane_copy(j).wait_send())
    loop(1, chips, lambda j: spread_copy(j).wait_send())
    over_chips(0, chips, owner_at, lambda j, q, to: ask(j, q, to).wait_send())
    for part in range(2):
        over_chips(
            0, chips, owner_at, lambda j, q, to: back_copy(part, j, q, to).wait_send()
        )
    arrive(rel_sum.at[pl.ds((1 - core) * by_core, by_core)], core_recv.at[1])

    def lay(t):
        rel_out[:, lanes(t * LANES, LANES)] = rel_sum[pl.ds(t * per_tile, per_tile)].reshape(
            per_tile * 16, LANES
        )

    loop(0, tiles, lay)
    give.wait_send()
    for part in range(2):
        alls[part].finish()
    grad_out[...] = full[...]
    for part in range(2):
        alls[part].drain()


def adagrad_kernel(table, state, grad, new_table, new_state):
    g = grad[: table.shape[0]].astype(F32)
    fresh = state[...] + jnp.sum(g * g, 0, keepdims=True) * (1.0 / g.shape[0])
    new_state[...] = fresh
    new_table[...] = table[...] - g * (RATE / jnp.sqrt(fresh))


def adagrad(table, state, grad, tile):
    width, rows = table.shape
    wide = pl.BlockSpec((width, tile), lambda i: (0, i))
    thin = pl.BlockSpec((1, tile), lambda i: (0, i))
    new_table, new_state = pl.pallas_call(
        adagrad_kernel,
        grid=(pl.cdiv(rows, tile),),
        out_shape=(
            jax.ShapeDtypeStruct((width, rows), F32),
            jax.ShapeDtypeStruct((1, rows), F32),
        ),
        in_specs=[wide, thin, pl.BlockSpec((grad.shape[0], tile), lambda i: (0, i))],
        out_specs=(wide, thin),
        compiler_params=pltpu.CompilerParams(vmem_limit_bytes=VMEM_LIMIT),
    )(table, state[None], grad)
    return new_table.T, new_state.reshape(rows)


VM = pl.BlockSpec(memory_space=pltpu.VMEM)
HBM = pl.BlockSpec(memory_space=pl.ANY)


def on_device(
    entity_table, entity_state, phase_table, phase_state,
    pull_rows, head_slot, tail_slot, neg_slot, relation,
):
    owners, dps = lax.axis_size("owner"), lax.axis_size("dp")
    table, phase = entity_table.T, phase_table.T
    width, rows = table.shape
    narrow, nrel = phase.shape
    triples = head_slot.shape[1]
    neg = neg_slot.shape[2]
    slots = jnp.concatenate([head_slot, tail_slot, neg_slot.reshape(1, -1)], 1)
    uses = slots.shape[1]
    pulls = owners * LANES
    requests = pull_rows.reshape(owners, 1, LANES)
    dma = pltpu.SemaphoreType.DMA
    chips = owners // 2
    padded = -(-narrow // 16) * 16
    units = -(-(nrel // LANES * padded // 16) // (8 * chips)) * 8 * chips
    biggest = -(-width // 64) * 16
    piece = units // 8 // chips
    grad, rel_total = pl.pallas_call(
        functools.partial(step_kernel, owners, triples // 2, neg),
        out_shape=(
            jax.ShapeDtypeStruct((width, rows), BF16),
            jax.ShapeDtypeStruct((padded, nrel), BF16),
        ),
        in_specs=[HBM, HBM, VM, VM, VM],
        out_specs=(VM, VM),
        scratch_shapes=[
            pltpu.VMEM((width, rows), F32),
            pltpu.VMEM((narrow, nrel), F32),
            pltpu.VMEM((width, rows), BF16),
            pltpu.VMEM((owners, 1, LANES), jnp.int32),
            pltpu.VMEM((1, pulls), jnp.int32),
            pltpu.VMEM((owners, width, LANES), BF16),
            pltpu.VMEM((width, pulls), BF16),
            pltpu.VMEM((width, uses), BF16),
            pltpu.VMEM((width, uses), BF16),
            pltpu.VMEM((width, triples), F32),
            pltpu.VMEM((narrow, triples), F32),
            pltpu.VMEM((narrow, triples), F32),
            pltpu.VMEM((padded, triples), F32),
            pltpu.VMEM((width, pulls), BF16),
            pltpu.VMEM((width, rows), F32),
            pltpu.VMEM((width, rows), BF16),
            pltpu.VMEM((2, 6, biggest, rows // 4), BF16),
            pltpu.VMEM((width, rows), BF16),
            pltpu.VMEM((units, 16, LANES), BF16),
            pltpu.VMEM((units // 2, 16, LANES), BF16),
            pltpu.VMEM((chips, 4, piece, 16, LANES), BF16),
            pltpu.VMEM((6, chips // 2, piece, 16, LANES), BF16),
            pltpu.VMEM((chips, piece, 16, LANES), BF16),
            pltpu.VMEM((units, 16, LANES), BF16),
            dma((2,)),
            dma((owners,)), dma((owners,)), dma((owners,)), dma((owners,)),
            dma((2, owners)), dma((2, owners)),
            dma((2, 6)), dma((2, 6)), dma((2, 6)), dma((2, 6)),
            dma((2,)), dma((2,)), dma((6,)), dma((6,)), dma((chips,)), dma((chips,)),
            dma((chips,)), dma((chips,)), dma((3,)), dma((3,)),
        ],
        compiler_params=pltpu.CompilerParams(
            collective_id=0, has_side_effects=True, vmem_limit_bytes=VMEM_LIMIT
        ),
        name="step",
    )(table, phase, requests, slots, relation)
    new_entity, new_entity_state = adagrad(table, entity_state, grad, 512)
    new_phase, new_phase_state = adagrad(phase, phase_state, rel_total, 1024)
    return (new_entity, new_entity_state, new_phase, new_phase_state)


def solution(mesh):
    placed = (
        P("owner", None),
        P("owner"),
        P(),
        P(),
        P(("owner", "dp"), None, None),
        P(("owner", "dp"), None),
        P(("owner", "dp"), None),
        P(("owner", "dp"), None, None),
        P(("owner", "dp"), None),
    )
    return jax.shard_map(
        on_device,
        mesh=mesh,
        in_specs=placed,
        out_specs=(P("owner", None), P("owner"), P(), P()),
        check_vma=False,
    )
```

```python
import functools

import jax
import jax.numpy as jnp
from jax import lax
from jax.experimental import pallas as pl
from jax.experimental.pallas import tpu as pltpu
from jax.sharding import PartitionSpec as P

GAMMA = 2.0
RATE = 0.05
LANES = 128
PAIR = 256
BF16 = jnp.bfloat16
F32 = jnp.float32
MESH = pl.DeviceIdType.MESH
VMEM_LIMIT = 60 * 2**20
NT = (((1,), (1,)), ((), ()))
TN = (((0,), (0,)), ((), ()))


def one_hot(rows, base, index):
    at = lax.broadcasted_iota(jnp.int32, (rows, index.shape[1]), 0) + base
    return jnp.where(at == index, 1.0, 0.0).astype(BF16)


def lanes(start, size):
    return pl.ds(pl.multiple_of(start, LANES), size)


def grid_of(owners):
    chips = owners // 2
    along_y = min(4, chips)
    return chips // along_y, along_y


def partner(me, j, nx, ny, back):
    chip = lax.div(me, 2)
    x, y = lax.div(chip, ny), lax.rem(chip, ny)
    if isinstance(j, int):
        dx = j % nx
        dy = (j // nx + dx) % ny
    else:
        dx = lax.rem(j, nx)
        dy = lax.rem(lax.div(j, nx) + dx, ny)
    x = lax.rem(x + (1 - 2 * back) * dx + back * nx, nx)
    y = lax.rem(y + (1 - 2 * back) * dy + back * ny, ny)
    return (x * ny + y) * 2


def positions(slots, me, nx, ny):
    chip = slots >> 8
    way = 1 - 2 * ((slots >> 7) & 1)
    x, y = chip // ny, chip & (ny - 1)
    mine = me // 2
    dx = (way * (mine // ny - x)) & (nx - 1)
    dy = (way * (mine % ny - y)) & (ny - 1)
    j = ((dy - dx) & (ny - 1)) * nx + dx
    return j * PAIR + (slots & (PAIR - 1))


def as_column(row):
    return jnp.broadcast_to(row, (LANES, row.shape[1])).T[:, :1]


def as_row(column):
    return jnp.broadcast_to(column, (column.shape[0], LANES)).T[:1, :]


def greet(me, owners, dp_me, dps):
    barrier = pltpu.get_barrier_semaphore()

    def hello(k, _):
        pl.semaphore_signal(
            barrier, inc=1, device_id={"owner": (me + k) % owners}, device_id_type=MESH
        )
        return 0

    lax.fori_loop(1, owners, hello, 0)
    for k in range(1, dps):
        pl.semaphore_signal(
            barrier, inc=1, device_id={"dp": (dp_me + k) % dps}, device_id_type=MESH
        )
    pl.semaphore_wait(barrier, owners - 1 + dps - 1)


def block_grads(b, group, neg, used, cosine, sine, grads, phase_grads):
    triples = 2 * group
    cols = lanes(b * group, group)
    tail_cols = lanes(triples + b * group, group)
    neg_cols = lanes(2 * triples + b * neg, neg)
    cos, sin = cosine[:, cols], sine[:, cols]
    width = cos.shape[0]
    heads = used[:, cols].astype(F32)
    head_re, head_im = heads[:width], heads[width:]
    rot_re = head_re * cos - head_im * sin
    rot_im = head_re * sin + head_im * cos
    rotated = jnp.concatenate([rot_re, rot_im], 0)
    diff = rotated - used[:, tail_cols].astype(F32)
    pos_score = GAMMA - jnp.sum(diff * diff, 0, keepdims=True)
    rot_half = rotated.astype(BF16)
    rot_wide = rot_half.astype(F32)
    negs = used[:, neg_cols]
    neg_wide = negs.astype(F32)
    row_norm = as_column(jnp.sum(rot_wide * rot_wide, 0, keepdims=True))
    neg_norm = jnp.sum(neg_wide * neg_wide, 0, keepdims=True)
    cross = lax.dot_general(rot_half, negs, TN, preferred_element_type=F32)
    neg_score = GAMMA - (row_norm + neg_norm - 2.0 * cross)
    weight = jax.nn.sigmoid(neg_score) * (1.0 / neg)
    weight_half = weight.astype(BF16)
    diff_grad = (2.0 * jax.nn.sigmoid(-pos_score)) * diff
    row_sum = as_row(jnp.sum(weight, 1, keepdims=True))
    col_sum = jnp.sum(weight, 0, keepdims=True)
    rot_grad = (
        diff_grad
        - (2.0 * row_sum) * rot_wide
        + 2.0 * lax.dot_general(negs, weight_half, NT, preferred_element_type=F32)
    )
    grads[:, neg_cols] = (
        2.0 * jnp.dot(rot_half, weight_half, preferred_element_type=F32)
        - (2.0 * col_sum) * neg_wide
    ).astype(BF16)
    grads[:, tail_cols] = (-diff_grad).astype(BF16)
    grad_re, grad_im = rot_grad[:width], rot_grad[width:]
    phase_grads[:width, cols] = grad_im * rot_re - grad_re * rot_im
    grads[:, cols] = jnp.concatenate(
        [grad_re * cos + grad_im * sin, grad_im * cos - grad_re * sin], 0
    ).astype(BF16)


def arrive(ref, sem):
    pltpu.make_async_copy(ref, ref, sem).wait()


class RingSum:
    def __init__(self, dp_me, piece, landing, send, recv):
        self.piece, self.landing, self.send, self.recv = piece, landing, send, recv
        self.me, self.right, self.left = dp_me, (dp_me + 1) % 4, (dp_me + 3) % 4
        self.opposite = (dp_me + 2) % 4

    def copy(self, src, slot, to):
        return pltpu.make_async_remote_copy(
            src_ref=src, dst_ref=self.landing[slot],
            send_sem=self.send.at[slot], recv_sem=self.recv.at[slot],
            device_id={"dp": to}, device_id_type=MESH,
        )

    def part(self, slot):
        z, h, to = (
            (self.opposite, 0, self.right),
            (self.opposite, 1, self.left),
            (self.right, 1, self.right),
            (self.left, 0, self.left),
            (self.right, 0, self.right),
            (self.left, 1, self.left),
        )[slot]
        return self.copy(self.piece(z, h), slot, to)

    def begin(self):
        for slot in range(4):
            self.part(slot).start()

    def relay(self):
        for slot, z, h in ((0, self.right, 0), (1, self.left, 1)):
            arrive(self.landing[slot], self.recv.at[slot])
            spot = self.piece(z, h)
            spot[...] = (spot[...].astype(F32) + self.landing[slot][...].astype(F32)).astype(BF16)
            self.part(4 + slot).start()

    def finish(self, h):
        slots = (4, 3) if h == 0 else (5, 2)
        for slot in slots:
            arrive(self.landing[slot], self.recv.at[slot])
        return self.landing[slots[0]][...].astype(F32) + self.landing[slots[1]][...].astype(F32)

    def drain(self):
        for slot in range(6):
            self.part(slot).wait_send()


class RingGather:
    def __init__(self, me, count, device, piece, send, recv):
        self.device, self.piece, self.send, self.recv = device, piece, send, recv
        self.count = count
        self.me, self.right, self.left = me, (me + 1) % count, (me + count - 1) % count
        self.opposite = (me + 2) % count

    def part(self, slot):
        z, h, to = (
            (self.me, 0, self.right),
            (self.me, 1, self.left),
            (self.me, 1, self.right),
            (self.me, 0, self.left),
            (self.left, 0, self.right),
            (self.right, 1, self.left),
        )[slot]
        return pltpu.make_async_remote_copy(
            src_ref=self.piece(z, h), dst_ref=self.piece(z, h),
            send_sem=self.send.at[slot], recv_sem=self.recv.at[slot],
            device_id=self.device(to), device_id_type=MESH,
        )

    def begin(self):
        if self.count == 4:
            for slot in range(4):
                self.part(slot).start()

    def relay(self):
        if self.count == 4:
            arrive(self.piece(self.left, 0), self.recv.at[0])
            self.part(4).start()
            arrive(self.piece(self.right, 1), self.recv.at[1])
            self.part(5).start()

    def finish(self):
        if self.count == 4:
            arrive(self.piece(self.left, 1), self.recv.at[2])
            arrive(self.piece(self.right, 0), self.recv.at[3])
            arrive(self.piece(self.opposite, 0), self.recv.at[4])
            arrive(self.piece(self.opposite, 1), self.recv.at[5])

    def drain(self):
        if self.count == 4:
            for slot in range(6):
                self.part(slot).wait_send()


class DirectGather:
    def __init__(self, me, count, device, piece, send, recv):
        self.me, self.count, self.device, self.piece = me, count, device, piece
        self.send, self.recv = send, recv

    def part(self, k):
        return pltpu.make_async_remote_copy(
            src_ref=self.piece(self.me), dst_ref=self.piece(self.me),
            send_sem=self.send.at[k - 1], recv_sem=self.recv.at[k - 1],
            device_id=self.device((self.me + k) % self.count), device_id_type=MESH,
        )

    def begin(self):
        for k in range(1, self.count):
            self.part(k).start()

    def finish(self):
        for k in range(1, self.count):
            source = (self.me + self.count - k) % self.count
            arrive(self.piece(source), self.recv.at[k - 1])

    def drain(self):
        for k in range(1, self.count):
            self.part(k).wait_send()


def cut_parts(features):
    units = features // 16
    counts = (10, 9, 6) if units == 25 else (units - 4, 2, 2)
    bounds = [0]
    for count in counts:
        bounds.append(bounds[-1] + 16 * count)
    return tuple(zip(bounds[:-1], bounds[1:]))


def split_part(low, high):
    cut = low + -(-(high - low) // 32) * 16
    return ((low, cut - low), (cut, high - cut))


def step_kernel(
    owners, group, neg,
    table_hbm, phase_hbm, requests, slots, relation,
    grad_out, rel_out,
    table, phase, table_half, asked, asked_column, sent, pulled, used, grads,
    theta, cosine, sine, phase_grads,
    received, total, shared, dp_in, full,
    raw, relations, share_sum, plane_in, rel_sum,
    load_sems, ask_send, ask_recv, row_send, row_recv, back_send, back_recv,
    dp_send, dp_recv, all_send, all_recv,
    core_send, core_recv, index_send, index_recv, raw_send, raw_recv,
    plane_send, plane_recv, piece_send, piece_recv,
    line_send, line_recv, sheet_send, sheet_recv,
):
    nx, ny = grid_of(owners)
    chips = nx * ny
    me = lax.axis_index("owner")
    dp_me = lax.axis_index("dp")
    core = me % 2
    load_table = pltpu.make_async_copy(table_hbm, table, load_sems.at[0])
    load_phase = pltpu.make_async_copy(phase_hbm, phase, load_sems.at[1])
    load_table.start()
    load_phase.start()
    greet(me, owners, dp_me, 4)

    def owner_at(j, q):
        return partner(me, j, nx, ny, 1 - q) + q

    def worker_at(j, q):
        return partner(me, j, nx, ny, core) + q

    def each_core(j, place_of, start, start_own):
        for q in range(2):
            to = place_of(j, q)
            if isinstance(j, int) and j == 0:
                pl.when(to != me)(functools.partial(start, j, q, to))
                pl.when(to == me)(functools.partial(start_own, q))
            else:
                start(j, q, to)

    def sent_all(ref, sem):
        arrive(ref.at[pl.ds(0, owners - 1)], sem)

    def loop(low, high, act):
        def body(j, _):
            act(j)
            return 0

        lax.fori_loop(low, high, body, 0)

    def ask(j, q, to):
        pltpu.make_async_remote_copy(
            src_ref=requests.at[to], dst_ref=asked.at[2 * j + core],
            send_sem=ask_send, recv_sem=ask_recv,
            device_id={"owner": to}, device_id_type=MESH,
        ).start()

    def ask_own(q):
        pltpu.make_async_copy(requests.at[me], asked.at[q], ask_recv).start()

    for j in range(chips):
        each_core(j, owner_at, ask, ask_own)

    def at_dp(z):
        return {"dp": z}

    relations[core, dp_me] = relation[...]
    indices = DirectGather(
        dp_me, 4, at_dp, lambda z: relations.at[core, z], index_send, index_recv
    )
    indices.begin()
    load_table.wait()
    table_half[...] = table[...].astype(BF16)

    cuts = (0, chips // 2, chips - chips // 4, chips)

    def row_copy(cut, j, q, to):
        pltpu.make_async_remote_copy(
            src_ref=sent.at[2 * j + q],
            dst_ref=pulled.at[:, lanes(j * PAIR + core * LANES, LANES)],
            send_sem=row_send, recv_sem=row_recv.at[cut],
            device_id={"owner": to}, device_id_type=MESH,
        ).start()

    def row_own(q):
        pltpu.make_async_copy(
            sent.at[q], pulled.at[:, q * LANES : (q + 1) * LANES], row_recv.at[0]
        ).start()

    def fetch(cut, j):
        wanted = jnp.concatenate([asked[2 * j], asked[2 * j + 1]], 1)
        asked_column[pl.ds(pl.multiple_of(j * PAIR, PAIR), PAIR)] = jnp.broadcast_to(
            wanted, (LANES, PAIR)
        ).T
        rows = jnp.dot(
            table_half[...], one_hot(table_half.shape[1], 0, wanted), preferred_element_type=F32
        ).astype(BF16)
        for q in range(2):
            sent[2 * j + q] = rows[:, q * LANES : (q + 1) * LANES]
        each_core(j, worker_at, functools.partial(row_copy, cut), row_own)

    arrive(asked, ask_recv)
    fetch(0, 0)
    for cut in range(3):
        loop(max(1, cuts[cut]), cuts[cut + 1], functools.partial(fetch, cut))

    load_phase.wait()
    rel_index = relation[...]
    nrel = phase.shape[1]
    width = phase.shape[0]
    step = 1024
    whole = nrel // step

    def phase_part(start, size):
        part = phase[:, lanes(start, size)]
        high = part.astype(BF16).astype(F32)
        both = jnp.concatenate([high, part - high], 0).astype(BF16)
        return jnp.dot(both, one_hot(size, start, rel_index), preferred_element_type=F32)

    theta[...] = jnp.zeros_like(theta)

    def add_phase(k, _):
        theta[...] += phase_part(k * step, step)
        return 0

    lax.fori_loop(0, whole, add_phase, 0)
    if nrel % step:
        theta[...] += phase_part(whole * step, nrel % step)
    angle = theta[:width] + theta[width:]
    cosine[...] = jnp.cos(angle)
    sine[...] = jnp.sin(angle)

    place = positions(slots[...], me, nx, ny)
    uses = slots.shape[1]
    tile = 256
    for cut in range(3):
        low, high = cuts[cut], cuts[cut + 1]
        if low == high:
            continue
        arrive(pulled.at[:, low * PAIR : high * PAIR], row_recv.at[cut])
        for t in range(uses // tile):
            cols = slice(t * tile, (t + 1) * tile)
            found = jnp.dot(
                pulled[:, low * PAIR : high * PAIR],
                one_hot((high - low) * PAIR, low * PAIR, place[:, cols]),
                preferred_element_type=F32,
            ).astype(BF16)
            used[:, cols] = found if low == 0 else used[:, cols] + found

    phase_grads[width:] = jnp.zeros_like(phase_grads[width:])
    for b in range(2):
        block_grads(b, group, neg, used, cosine, sine, grads, phase_grads)

    raw[core, dp_me] = phase_grads[...].astype(BF16)
    padded = raw.shape[2]
    raw_halves = split_part(0, padded)
    raw_ring = RingGather(
        dp_me, 4, at_dp, lambda z, h: raw.at[core, z, pl.ds(*raw_halves[h])],
        raw_send, raw_recv,
    )
    raw_ring.begin()
    sibling = me + 1 - 2 * core

    def to_sibling(ref, slot):
        return pltpu.make_async_remote_copy(
            src_ref=ref.at[core], dst_ref=ref.at[core],
            send_sem=core_send.at[slot], recv_sem=core_recv.at[slot],
            device_id={"owner": sibling}, device_id_type=MESH,
        )

    per_tile = padded // 16
    share_tiles = -(-(nrel // LANES) // 16) * 2
    by_piece = rel_sum.shape[4]
    chip = me // 2
    my_x, my_y = chip // ny, chip % ny
    eighth = core * 4 + dp_me

    def sum_share():
        base = eighth * share_tiles * LANES
        for t in range(share_tiles // 2):
            found = None
            for c in range(2):
                for z in range(4):
                    part = lax.dot_general(
                        raw[c, z], one_hot(PAIR, base + t * PAIR, relations[c, z]), NT,
                        preferred_element_type=F32,
                    )
                    found = part if found is None else found + part
            found = found.astype(BF16)
            for i in range(2):
                at = (2 * t + i) * per_tile
                share_sum[at : at + per_tile] = found[
                    :, i * LANES : (i + 1) * LANES
                ].reshape(per_tile, 16, LANES)
        filled = share_tiles * per_tile
        if filled < share_sum.shape[0]:
            share_sum[filled:] = jnp.zeros_like(share_sum[filled:])

    def plane_copy(j):
        to = partner(me, j, nx, ny, core)
        pltpu.make_async_remote_copy(
            src_ref=share_sum.at[pl.ds(lax.div(to, 2) * by_piece, by_piece)],
            dst_ref=plane_in.at[j], send_sem=plane_send, recv_sem=plane_recv,
            device_id={"owner": to + core}, device_id_type=MESH,
        ).start()

    def add_plane(j, value):
        return value + plane_in[j].astype(F32)

    pieces = DirectGather(
        dp_me, 4, at_dp, lambda z: rel_sum.at[core, my_x, my_y, z], piece_send, piece_recv
    )

    def at_x(x):
        return {"owner": (x * ny + my_y) * 2 + core}

    def at_y(y):
        return {"owner": (my_x * ny + y) * 2 + core}

    low_z, high_z = pl.ds(0, 2), pl.ds(2, 2)
    lines = (
        DirectGather(
            my_x, nx, at_x, lambda x: rel_sum.at[core, x, my_y, low_z],
            line_send.at[0], line_recv.at[0],
        ),
        DirectGather(
            my_y, ny, at_y, lambda y: rel_sum.at[core, my_x, y, high_z],
            line_send.at[1], line_recv.at[1],
        ),
    )

    def two(h):
        return pl.ds(2 * h, 2)

    sheets = (
        RingGather(
            my_y, ny, at_y,
            lambda y, h: rel_sum.at[core, two(h) if nx == 4 else slice(None), y,
                                    low_z if nx == 4 else pl.ds(h, 1)],
            sheet_send.at[0], sheet_recv.at[0],
        ),
        RingGather(
            my_x, nx, at_x, lambda x, h: rel_sum.at[core, x, two(h), high_z],
            sheet_send.at[1], sheet_recv.at[1],
        ),
    )

    sent_all(sent, row_send)
    parts = cut_parts(total.shape[0])
    numbers = range(len(parts))

    def back_copy(part, j, q, to):
        low, high = parts[part]
        pltpu.make_async_remote_copy(
            src_ref=sent.at[2 * j + q, pl.ds(low, high - low)],
            dst_ref=received.at[pl.ds(low, high - low), lanes(j * PAIR + core * LANES, LANES)],
            send_sem=back_send.at[part], recv_sem=back_recv.at[part],
            device_id={"owner": to}, device_id_type=MESH,
        ).start()

    def back_own(part, q):
        low, high = parts[part]
        pltpu.make_async_copy(
            sent.at[q, pl.ds(low, high - low)],
            received.at[pl.ds(low, high - low), q * LANES : (q + 1) * LANES],
            back_recv.at[part],
        ).start()

    def push(j):
        sums = lax.dot_general(
            grads[...], one_hot(PAIR, j * PAIR, place), NT, preferred_element_type=F32
        ).astype(BF16)
        for q in range(2):
            sent[2 * j + q] = sums[:, q * LANES : (q + 1) * LANES]
        send_back(0, j)

    def send_back(part, j):
        each_core(
            j, owner_at, functools.partial(back_copy, part), functools.partial(back_own, part)
        )

    def send_later(part):
        for j in range(chips):
            send_back(part, j)

    first, second, third = min(3, chips), min(7, chips), min(10, chips)
    push(0)
    loop(1, first, push)
    indices.finish()
    raw_ring.relay()
    loop(first, second, push)
    raw_ring.finish()
    to_sibling(raw, 0).start()
    to_sibling(relations, 1).start()
    loop(second, third, push)
    loop(third, chips, push)
    send_later(1)
    arrive(raw.at[1 - core], core_recv.at[0])
    arrive(relations.at[1 - core], core_recv.at[1])
    sum_share()
    for j in range(1, chips):
        plane_copy(j)

    rows = total.shape[1]
    share = rows // 4

    def scatter(part, between):
        low, high = parts[part]
        count = rows // tile
        arrive(received.at[low:high], back_recv.at[part])
        for t in range(count):
            for at, act in between:
                if at * count // 8 == t:
                    act()
            cols = slice(t * tile, (t + 1) * tile)
            row = lax.broadcasted_iota(jnp.int32, (received.shape[1], tile), 1) + t * tile
            wanted = jnp.concatenate([asked_column[...]] * (tile // LANES), 1)
            added = jnp.dot(
                received[low:high], jnp.where(wanted == row, 1.0, 0.0).astype(BF16),
                preferred_element_type=F32,
            )
            total[low:high, cols] = added
            shared[low:high, cols] = added.astype(BF16)

    def halves(part):
        return split_part(*parts[part])

    def piece_of(ref, part):
        return lambda z, h: ref.at[pl.ds(*halves(part)[h]), lanes(z * share, share)]

    def dp_sum(part):
        sizes = [halves(part)[h][1] for h in (0, 1, 1, 0, 0, 1)]
        return RingSum(
            dp_me, piece_of(shared, part),
            [dp_in.at[part, i, pl.ds(0, sizes[i])] for i in range(6)],
            dp_send.at[part], dp_recv.at[part],
        )

    sums = [dp_sum(part) for part in numbers]
    alls = [
        RingGather(
            dp_me, 4, at_dp, piece_of(full, part), all_send.at[part], all_recv.at[part]
        )
        for part in numbers
    ]

    def settle(part):
        for h in range(2):
            own = piece_of(total, part)(dp_me, h)
            alls[part].piece(dp_me, h)[...] = (own[...] + sums[part].finish(h)).astype(BF16)
        alls[part].begin()

    def sum_plane():
        mine = share_sum.at[pl.ds(chip * by_piece, by_piece)]
        arrive(plane_in.at[1:], plane_recv)
        rel_sum[core, my_x, my_y, dp_me] = lax.fori_loop(
            1, chips, add_plane, mine[...].astype(F32)
        ).astype(BF16)
        pieces.begin()

    def start_lines():
        pieces.finish()
        for line in lines:
            line.begin()

    def start_sheets():
        for line in lines:
            line.finish()
        for ring in sheets:
            ring.begin()

    def relay_sheets():
        for ring in sheets:
            ring.relay()

    def start_core():
        for ring in sheets:
            ring.finish()
        to_sibling(rel_sum, 2).start()

    scatter(0, [(6, functools.partial(send_later, 2)), (7, sum_plane)])
    sums[0].begin()
    start_lines()
    scatter(1, [(2, sums[0].relay), (4, start_sheets)])
    sums[1].begin()
    scatter(2, [
        (0, functools.partial(settle, 0)), (1, relay_sheets), (4, sums[1].relay),
        (5, alls[0].relay), (7, start_core),
    ])
    sums[2].begin()
    last = 2

    def lay(c, z):
        for unit in range(share_tiles * per_tile):
            p, i = unit // by_piece, unit % by_piece
            t, r = unit // per_tile, unit % per_tile
            cols = lanes(((c * 4 + z) * share_tiles + t) * LANES, LANES)
            rel_out[16 * r : 16 * r + 16, cols] = rel_sum[c, p // ny, p % ny, z, i]

    settle(1)
    sums[last].relay()
    loop(0, 4, lambda z: lay(core, z))
    alls[1].relay()
    settle(last)
    arrive(rel_sum.at[1 - core], core_recv.at[2])
    loop(0, 4, lambda z: lay(1 - core, z))
    alls[last].relay()

    indices.drain()
    raw_ring.drain()
    to_sibling(raw, 0).wait_send()
    to_sibling(relations, 1).wait_send()
    to_sibling(rel_sum, 2).wait_send()
    pieces.drain()
    for gather in lines + sheets:
        gather.drain()
    for part in numbers:
        sums[part].drain()
    arrive(plane_in.at[1:], plane_send)
    sent_all(asked, ask_send)
    for part, (low, high) in enumerate(parts):
        sent_all(sent.at[:, low:high], back_send.at[part])
    for part in numbers:
        alls[part].finish()
    grad_out[...] = full[...]
    for part in numbers:
        alls[part].drain()


def chunks_of(rows, size):
    return [(start, min(size, rows - start)) for start in range(0, rows, size)]


def adagrad_kernel(
    cuts, table, state, grad, phase, phase_state, rel_grad,
    new_table, new_state, new_phase, new_phase_state,
    table_now, grad_now, phase_now, rel_now, table_in, grad_in, out_sems,
):
    jobs = [
        (table, grad, table_now, grad_now, state, new_table, new_state, start, size)
        for start, size in cuts[0]
    ] + [
        (phase, rel_grad, phase_now, rel_now, phase_state, new_phase, new_phase_state, start, size)
        for start, size in cuts[1]
    ]

    def load(i):
        source, gradient, now, grad_at, _, _, _, start, size = jobs[i]
        cols = pl.ds(start, size)
        return (
            pltpu.make_async_copy(source.at[:, cols], now.at[:, cols], table_in.at[i]),
            pltpu.make_async_copy(gradient.at[:, cols], grad_at.at[:, cols], grad_in.at[i]),
        )

    def store(i):
        _, _, now, _, _, target, _, start, size = jobs[i]
        cols = pl.ds(start, size)
        return pltpu.make_async_copy(now.at[:, cols], target.at[:, cols], out_sems.at[i])

    for i in range(len(jobs)):
        for copy in load(i):
            copy.start()
    for i, (_, _, now, grad_at, old, _, new, start, size) in enumerate(jobs):
        for copy in load(i):
            copy.wait()
        cols = pl.ds(start, size)
        g = grad_at[: now.shape[0], cols].astype(F32)
        fresh = old[:, cols] + jnp.sum(g * g, 0, keepdims=True) * (1.0 / g.shape[0])
        new[:, cols] = fresh
        now[:, cols] = now[:, cols] - g * (RATE / jnp.sqrt(fresh))
        store(i).start()
    for i in range(len(jobs)):
        store(i).wait()


def adagrad(table, state, grad, phase, phase_state, rel_grad):
    width, rows = table.shape
    narrow, nrel = phase.shape
    cuts = (chunks_of(rows, 512), chunks_of(nrel, 1024))
    count = len(cuts[0]) + len(cuts[1])
    dma = pltpu.SemaphoreType.DMA
    new_table, new_state, new_phase, new_phase_state = pl.pallas_call(
        functools.partial(adagrad_kernel, cuts),
        out_shape=(
            jax.ShapeDtypeStruct((width, rows), F32),
            jax.ShapeDtypeStruct((1, rows), F32),
            jax.ShapeDtypeStruct((narrow, nrel), F32),
            jax.ShapeDtypeStruct((1, nrel), F32),
        ),
        in_specs=[HBM, VM, HBM, HBM, VM, HBM],
        out_specs=(HBM, VM, HBM, VM),
        scratch_shapes=[
            pltpu.VMEM((width, rows), F32),
            pltpu.VMEM((width, rows), BF16),
            pltpu.VMEM((narrow, nrel), F32),
            pltpu.VMEM(rel_grad.shape, BF16),
            dma((count,)), dma((count,)), dma((count,)),
        ],
        compiler_params=pltpu.CompilerParams(vmem_limit_bytes=VMEM_LIMIT),
        name="adagrad",
    )(table, state[None], grad, phase, phase_state[None], rel_grad)
    return new_table.T, new_state.reshape(rows), new_phase.T, new_phase_state.reshape(nrel)


VM = pl.BlockSpec(memory_space=pltpu.VMEM)
HBM = pl.BlockSpec(memory_space=pl.ANY)


def on_device(
    entity_table, entity_state, phase_table, phase_state,
    pull_rows, head_slot, tail_slot, neg_slot, relation,
):
    owners, dps = lax.axis_size("owner"), lax.axis_size("dp")
    table, phase = entity_table.T, phase_table.T
    width, rows = table.shape
    narrow, nrel = phase.shape
    triples = head_slot.shape[1]
    neg = neg_slot.shape[2]
    slots = jnp.concatenate([head_slot, tail_slot, neg_slot.reshape(1, -1)], 1)
    uses = slots.shape[1]
    pulls = owners * LANES
    requests = pull_rows.reshape(owners, 1, LANES)
    dma = pltpu.SemaphoreType.DMA
    chips = owners // 2
    padded = -(-narrow // 16) * 16
    share_tiles = -(-(nrel // LANES) // 16) * 2
    piece = -(-(share_tiles * padded // 16) // chips)
    nx, ny = grid_of(owners)
    parts = len(cut_parts(width))
    biggest = max(split_part(*part)[0][1] for part in cut_parts(width))
    grad, rel_total = pl.pallas_call(
        functools.partial(step_kernel, owners, triples // 2, neg),
        out_shape=(
            jax.ShapeDtypeStruct((width, rows), BF16),
            jax.ShapeDtypeStruct((padded, 8 * share_tiles * LANES), BF16),
        ),
        in_specs=[HBM, HBM, VM, VM, VM],
        out_specs=(VM, VM),
        scratch_shapes=[
            pltpu.VMEM((width, rows), F32),
            pltpu.VMEM((narrow, nrel), F32),
            pltpu.VMEM((width, rows), BF16),
            pltpu.VMEM((owners, 1, LANES), jnp.int32),
            pltpu.VMEM((pulls, LANES), jnp.int32),
            pltpu.VMEM((owners, width, LANES), BF16),
            pltpu.VMEM((width, pulls), BF16),
            pltpu.VMEM((width, uses), BF16),
            pltpu.VMEM((width, uses), BF16),
            pltpu.VMEM((width, triples), F32),
            pltpu.VMEM((narrow, triples), F32),
            pltpu.VMEM((narrow, triples), F32),
            pltpu.VMEM((padded, triples), F32),
            pltpu.VMEM((width, pulls), BF16),
            pltpu.VMEM((width, rows), F32),
            pltpu.VMEM((width, rows), BF16),
            pltpu.VMEM((parts, 6, biggest, rows // 4), BF16),
            pltpu.VMEM((width, rows), BF16),
            pltpu.VMEM((2, 4, padded, triples), BF16),
            pltpu.VMEM((2, 4, 1, triples), jnp.int32),
            pltpu.VMEM((chips * piece, 16, LANES), BF16),
            pltpu.VMEM((chips, piece, 16, LANES), BF16),
            pltpu.VMEM((2, nx, ny, 4, piece, 16, LANES), BF16),
            dma((2,)),
            dma, dma, dma, dma((3,)), dma((parts,)), dma((parts,)),
            dma((parts, 6)), dma((parts, 6)), dma((parts, 6)), dma((parts, 6)),
            dma((3,)), dma((3,)), dma((3,)), dma((3,)), dma((6,)), dma((6,)),
            dma, dma, dma((3,)), dma((3,)),
            dma((2, 3)), dma((2, 3)), dma((2, 6)), dma((2, 6)),
        ],
        compiler_params=pltpu.CompilerParams(
            collective_id=0, has_side_effects=True, vmem_limit_bytes=VMEM_LIMIT
        ),
        name="step",
    )(table, phase, requests, slots, relation)
    return adagrad(table, entity_state, grad, phase, phase_state, rel_total)


def solution(mesh):
    placed = (
        P("owner", None),
        P("owner"),
        P(),
        P(),
        P(("owner", "dp"), None, None),
        P(("owner", "dp"), None),
        P(("owner", "dp"), None),
        P(("owner", "dp"), None, None),
        P(("owner", "dp"), None),
    )
    return jax.shard_map(
        on_device,
        mesh=mesh,
        in_specs=placed,
        out_specs=(P("owner", None), P("owner"), P(), P()),
        check_vma=False,
    )
```

```python
import functools

import jax
import jax.numpy as jnp
from jax import lax
from jax.experimental import pallas as pl
from jax.experimental.pallas import tpu as pltpu
from jax.sharding import PartitionSpec as P

GAMMA = 2.0
RATE = 0.05
LANES = 128
PAIR = 256
BF16 = jnp.bfloat16
F32 = jnp.float32
MESH = pl.DeviceIdType.MESH
VMEM_LIMIT = 60 * 2**20
NT = (((1,), (1,)), ((), ()))
TN = (((0,), (0,)), ((), ()))


def one_hot(rows, base, index):
    at = lax.broadcasted_iota(jnp.int32, (rows, index.shape[1]), 0) + base
    return jnp.where(at == index, 1.0, 0.0).astype(BF16)


def lanes(start, size):
    return pl.ds(pl.multiple_of(start, LANES), size)


def grid_of(owners):
    chips = owners // 2
    along_y = min(4, chips)
    return chips // along_y, along_y


def partner(me, j, nx, ny, back):
    chip = lax.div(me, 2)
    x, y = lax.div(chip, ny), lax.rem(chip, ny)
    if isinstance(j, int):
        dx = j % nx
        dy = (j // nx + dx) % ny
    else:
        dx = lax.rem(j, nx)
        dy = lax.rem(lax.div(j, nx) + dx, ny)
    x = lax.rem(x + (1 - 2 * back) * dx + back * nx, nx)
    y = lax.rem(y + (1 - 2 * back) * dy + back * ny, ny)
    return (x * ny + y) * 2


def positions(slots, me, nx, ny):
    chip = slots >> 8
    way = 1 - 2 * ((slots >> 7) & 1)
    x, y = chip // ny, chip & (ny - 1)
    mine = me // 2
    dx = (way * (mine // ny - x)) & (nx - 1)
    dy = (way * (mine % ny - y)) & (ny - 1)
    j = ((dy - dx) & (ny - 1)) * nx + dx
    return j * PAIR + (slots & (PAIR - 1))


def as_column(row):
    return jnp.broadcast_to(row, (LANES, row.shape[1])).T[:, :1]


def as_row(column):
    return jnp.broadcast_to(column, (column.shape[0], LANES)).T[:1, :]


def greet(me, owners, dp_me, dps):
    barrier = pltpu.get_barrier_semaphore()

    def hello(k, _):
        pl.semaphore_signal(
            barrier, inc=1, device_id={"owner": (me + k) % owners}, device_id_type=MESH
        )
        return 0

    lax.fori_loop(1, owners, hello, 0)
    for k in range(1, dps):
        pl.semaphore_signal(
            barrier, inc=1, device_id={"dp": (dp_me + k) % dps}, device_id_type=MESH
        )
    pl.semaphore_wait(barrier, owners - 1 + dps - 1)


def block_grads(b, group, neg, used, cosine, sine, grads, phase_grads):
    triples = 2 * group
    cols = lanes(b * group, group)
    tail_cols = lanes(triples + b * group, group)
    neg_cols = lanes(2 * triples + b * neg, neg)
    cos, sin = cosine[:, cols], sine[:, cols]
    width = cos.shape[0]
    heads = used[:, cols].astype(F32)
    head_re, head_im = heads[:width], heads[width:]
    rot_re = head_re * cos - head_im * sin
    rot_im = head_re * sin + head_im * cos
    rotated = jnp.concatenate([rot_re, rot_im], 0)
    diff = rotated - used[:, tail_cols].astype(F32)
    pos_score = GAMMA - jnp.sum(diff * diff, 0, keepdims=True)
    rot_half = rotated.astype(BF16)
    rot_wide = rot_half.astype(F32)
    negs = used[:, neg_cols]
    neg_wide = negs.astype(F32)
    row_norm = as_column(jnp.sum(rot_wide * rot_wide, 0, keepdims=True))
    neg_norm = jnp.sum(neg_wide * neg_wide, 0, keepdims=True)
    cross = lax.dot_general(rot_half, negs, TN, preferred_element_type=F32)
    neg_score = GAMMA - (row_norm + neg_norm - 2.0 * cross)
    weight = jax.nn.sigmoid(neg_score) * (1.0 / neg)
    weight_half = weight.astype(BF16)
    diff_grad = (2.0 * jax.nn.sigmoid(-pos_score)) * diff
    row_sum = as_row(jnp.sum(weight, 1, keepdims=True))
    col_sum = jnp.sum(weight, 0, keepdims=True)
    rot_grad = (
        diff_grad
        - (2.0 * row_sum) * rot_wide
        + 2.0 * lax.dot_general(negs, weight_half, NT, preferred_element_type=F32)
    )
    grads[:, neg_cols] = (
        2.0 * jnp.dot(rot_half, weight_half, preferred_element_type=F32)
        - (2.0 * col_sum) * neg_wide
    ).astype(BF16)
    grads[:, tail_cols] = (-diff_grad).astype(BF16)
    grad_re, grad_im = rot_grad[:width], rot_grad[width:]
    phase_grads[:width, cols] = grad_im * rot_re - grad_re * rot_im
    grads[:, cols] = jnp.concatenate(
        [grad_re * cos + grad_im * sin, grad_im * cos - grad_re * sin], 0
    ).astype(BF16)


def arrive(ref, sem):
    pltpu.make_async_copy(ref, ref, sem).wait()


class RingSum:
    def __init__(self, dp_me, piece, landing, send, recv):
        self.piece, self.landing, self.send, self.recv = piece, landing, send, recv
        self.me, self.right, self.left = dp_me, (dp_me + 1) % 4, (dp_me + 3) % 4
        self.opposite = (dp_me + 2) % 4

    def copy(self, src, slot, to):
        return pltpu.make_async_remote_copy(
            src_ref=src, dst_ref=self.landing[slot],
            send_sem=self.send.at[slot], recv_sem=self.recv.at[slot],
            device_id={"dp": to}, device_id_type=MESH,
        )

    def part(self, slot):
        z, h, to = (
            (self.opposite, 0, self.right),
            (self.opposite, 1, self.left),
            (self.right, 1, self.right),
            (self.left, 0, self.left),
            (self.right, 0, self.right),
            (self.left, 1, self.left),
        )[slot]
        return self.copy(self.piece(z, h), slot, to)

    def begin(self):
        for slot in range(4):
            self.part(slot).start()

    def relay(self):
        for slot, z, h in ((0, self.right, 0), (1, self.left, 1)):
            arrive(self.landing[slot], self.recv.at[slot])
            spot = self.piece(z, h)
            spot[...] = (spot[...].astype(F32) + self.landing[slot][...].astype(F32)).astype(BF16)
            self.part(4 + slot).start()

    def finish(self, h):
        slots = (4, 3) if h == 0 else (5, 2)
        for slot in slots:
            arrive(self.landing[slot], self.recv.at[slot])
        return self.landing[slots[0]][...].astype(F32) + self.landing[slots[1]][...].astype(F32)

    def drain(self):
        for slot in range(6):
            self.part(slot).wait_send()


class RingGather:
    def __init__(self, me, count, device, piece, send, recv):
        self.device, self.piece, self.send, self.recv = device, piece, send, recv
        self.count = count
        self.me, self.right, self.left = me, (me + 1) % count, (me + count - 1) % count
        self.opposite = (me + 2) % count

    def part(self, slot):
        z, h, to = (
            (self.me, 0, self.right),
            (self.me, 1, self.left),
            (self.me, 1, self.right),
            (self.me, 0, self.left),
            (self.left, 0, self.right),
            (self.right, 1, self.left),
        )[slot]
        return pltpu.make_async_remote_copy(
            src_ref=self.piece(z, h), dst_ref=self.piece(z, h),
            send_sem=self.send.at[slot], recv_sem=self.recv.at[slot],
            device_id=self.device(to), device_id_type=MESH,
        )

    def begin(self):
        if self.count == 4:
            for slot in range(4):
                self.part(slot).start()

    def relay(self):
        if self.count == 4:
            arrive(self.piece(self.left, 0), self.recv.at[0])
            self.part(4).start()
            arrive(self.piece(self.right, 1), self.recv.at[1])
            self.part(5).start()

    def finish(self):
        if self.count == 4:
            arrive(self.piece(self.left, 1), self.recv.at[2])
            arrive(self.piece(self.right, 0), self.recv.at[3])
            arrive(self.piece(self.opposite, 0), self.recv.at[4])
            arrive(self.piece(self.opposite, 1), self.recv.at[5])

    def drain(self):
        if self.count == 4:
            for slot in range(6):
                self.part(slot).wait_send()


class DirectGather:
    def __init__(self, me, count, device, piece, send, recv):
        self.me, self.count, self.device, self.piece = me, count, device, piece
        self.send, self.recv = send, recv

    def part(self, k):
        return pltpu.make_async_remote_copy(
            src_ref=self.piece(self.me), dst_ref=self.piece(self.me),
            send_sem=self.send.at[k - 1], recv_sem=self.recv.at[k - 1],
            device_id=self.device((self.me + k) % self.count), device_id_type=MESH,
        )

    def begin(self):
        for k in range(1, self.count):
            self.part(k).start()

    def finish(self):
        for k in range(1, self.count):
            source = (self.me + self.count - k) % self.count
            arrive(self.piece(source), self.recv.at[k - 1])

    def drain(self):
        for k in range(1, self.count):
            self.part(k).wait_send()


def cut_parts(features):
    units = features // 16
    counts = (10, 9, 6) if units == 25 else (units - 4, 2, 2)
    bounds = [0]
    for count in counts:
        bounds.append(bounds[-1] + 16 * count)
    return tuple(zip(bounds[:-1], bounds[1:]))


def split_part(low, high):
    cut = low + -(-(high - low) // 32) * 16
    return ((low, cut - low), (cut, high - cut))


def step_kernel(
    owners, group, neg,
    table_hbm, phase_hbm, requests, head_slot, tail_slot, neg_slot, relation,
    grad_out, rel_out,
    table, phase, table_half, asked, asked_column, sent, pulled, used, grads,
    theta, cosine, sine, phase_grads,
    received, total, shared, dp_in, full,
    raw, relations, share_sum, plane_in, rel_sum,
    load_sems, ask_send, ask_recv, row_send, row_recv, back_send, back_recv,
    dp_send, dp_recv, all_send, all_recv,
    core_send, core_recv, index_send, index_recv, raw_send, raw_recv,
    plane_send, plane_recv, piece_send, piece_recv,
    line_send, line_recv, sheet_send, sheet_recv,
):
    nx, ny = grid_of(owners)
    chips = nx * ny
    me = lax.axis_index("owner")
    dp_me = lax.axis_index("dp")
    core = me % 2
    load_table = pltpu.make_async_copy(table_hbm, table, load_sems.at[0])
    load_phase = pltpu.make_async_copy(phase_hbm, phase, load_sems.at[1])
    load_table.start()
    load_phase.start()
    greet(me, owners, dp_me, 4)

    def owner_at(j, q):
        return partner(me, j, nx, ny, 1 - q) + q

    def worker_at(j, q):
        return partner(me, j, nx, ny, core) + q

    def each_core(j, place_of, start, start_own):
        for q in range(2):
            to = place_of(j, q)
            if isinstance(j, int) and j == 0:
                pl.when(to != me)(functools.partial(start, j, q, to))
                pl.when(to == me)(functools.partial(start_own, q))
            else:
                start(j, q, to)

    def sent_all(ref, sem):
        arrive(ref.at[pl.ds(0, owners - 1)], sem)

    def loop(low, high, act):
        def body(j, _):
            act(j)
            return 0

        lax.fori_loop(low, high, body, 0)

    def ask(j, q, to):
        pltpu.make_async_remote_copy(
            src_ref=requests.at[to], dst_ref=asked.at[2 * j + core],
            send_sem=ask_send, recv_sem=ask_recv,
            device_id={"owner": to}, device_id_type=MESH,
        ).start()

    def ask_own(q):
        pltpu.make_async_copy(requests.at[me], asked.at[q], ask_recv).start()

    for j in range(chips):
        each_core(j, owner_at, ask, ask_own)

    def at_dp(z):
        return {"dp": z}

    relations[core, dp_me] = relation[...]
    indices = DirectGather(
        dp_me, 4, at_dp, lambda z: relations.at[core, z], index_send, index_recv
    )
    indices.begin()
    load_table.wait()
    table_half[...] = table[...].astype(BF16)

    cuts = (0, chips // 2, chips - chips // 4, chips)

    def row_copy(cut, j, q, to):
        pltpu.make_async_remote_copy(
            src_ref=sent.at[2 * j + q],
            dst_ref=pulled.at[:, lanes(j * PAIR + core * LANES, LANES)],
            send_sem=row_send, recv_sem=row_recv.at[cut],
            device_id={"owner": to}, device_id_type=MESH,
        ).start()

    def row_own(q):
        pltpu.make_async_copy(
            sent.at[q], pulled.at[:, q * LANES : (q + 1) * LANES], row_recv.at[0]
        ).start()

    def fetch(cut, j):
        wanted = jnp.concatenate([asked[2 * j], asked[2 * j + 1]], 1)
        asked_column[pl.ds(pl.multiple_of(j * PAIR, PAIR), PAIR)] = jnp.broadcast_to(
            wanted, (LANES, PAIR)
        ).T
        rows = jnp.dot(
            table_half[...], one_hot(table_half.shape[1], 0, wanted), preferred_element_type=F32
        ).astype(BF16)
        for q in range(2):
            sent[2 * j + q] = rows[:, q * LANES : (q + 1) * LANES]
        each_core(j, worker_at, functools.partial(row_copy, cut), row_own)

    arrive(asked, ask_recv)
    fetch(0, 0)
    for cut in range(3):
        loop(max(1, cuts[cut]), cuts[cut + 1], functools.partial(fetch, cut))

    load_phase.wait()
    rel_index = relation[...]
    nrel = phase.shape[1]
    width = phase.shape[0]
    step = 1024
    whole = nrel // step

    def phase_part(start, size):
        part = phase[:, lanes(start, size)]
        high = part.astype(BF16).astype(F32)
        both = jnp.concatenate([high, part - high], 0).astype(BF16)
        return jnp.dot(both, one_hot(size, start, rel_index), preferred_element_type=F32)

    theta[...] = jnp.zeros_like(theta)

    def add_phase(k, _):
        theta[...] += phase_part(k * step, step)
        return 0

    lax.fori_loop(0, whole, add_phase, 0)
    if nrel % step:
        theta[...] += phase_part(whole * step, nrel % step)
    angle = theta[:width] + theta[width:]
    cosine[...] = jnp.cos(angle)
    sine[...] = jnp.sin(angle)

    slots = [head_slot[...], tail_slot[...]]
    slots += [neg_slot[0, b : b + 1] for b in range(neg_slot.shape[1])]
    place = positions(jnp.concatenate(slots, 1), me, nx, ny)
    uses = place.shape[1]
    tile = 256
    for cut in range(3):
        low, high = cuts[cut], cuts[cut + 1]
        if low == high:
            continue
        arrive(pulled.at[:, low * PAIR : high * PAIR], row_recv.at[cut])
        for t in range(uses // tile):
            cols = slice(t * tile, (t + 1) * tile)
            found = jnp.dot(
                pulled[:, low * PAIR : high * PAIR],
                one_hot((high - low) * PAIR, low * PAIR, place[:, cols]),
                preferred_element_type=F32,
            ).astype(BF16)
            used[:, cols] = found if low == 0 else used[:, cols] + found

    phase_grads[width:] = jnp.zeros_like(phase_grads[width:])
    for b in range(2):
        block_grads(b, group, neg, used, cosine, sine, grads, phase_grads)

    raw[core, dp_me] = phase_grads[...].astype(BF16)
    padded = raw.shape[2]
    raw_halves = split_part(0, padded)
    raw_ring = RingGather(
        dp_me, 4, at_dp, lambda z, h: raw.at[core, z, pl.ds(*raw_halves[h])],
        raw_send, raw_recv,
    )
    raw_ring.begin()
    sibling = me + 1 - 2 * core

    def to_sibling(ref, slot):
        return pltpu.make_async_remote_copy(
            src_ref=ref.at[core], dst_ref=ref.at[core],
            send_sem=core_send.at[slot], recv_sem=core_recv.at[slot],
            device_id={"owner": sibling}, device_id_type=MESH,
        )

    per_tile = padded // 16
    share_tiles = -(-(nrel // LANES) // 16) * 2
    by_piece = rel_sum.shape[4]
    chip = me // 2
    my_x, my_y = chip // ny, chip % ny
    eighth = core * 4 + dp_me

    def sum_share():
        base = eighth * share_tiles * LANES
        for t in range(share_tiles // 2):
            found = None
            for c in range(2):
                for z in range(4):
                    part = lax.dot_general(
                        raw[c, z], one_hot(PAIR, base + t * PAIR, relations[c, z]), NT,
                        preferred_element_type=F32,
                    )
                    found = part if found is None else found + part
            found = found.astype(BF16)
            for i in range(2):
                at = (2 * t + i) * per_tile
                share_sum[at : at + per_tile] = found[
                    :, i * LANES : (i + 1) * LANES
                ].reshape(per_tile, 16, LANES)
        filled = share_tiles * per_tile
        if filled < share_sum.shape[0]:
            share_sum[filled:] = jnp.zeros_like(share_sum[filled:])

    def plane_copy(j):
        to = partner(me, j, nx, ny, core)
        pltpu.make_async_remote_copy(
            src_ref=share_sum.at[pl.ds(lax.div(to, 2) * by_piece, by_piece)],
            dst_ref=plane_in.at[j], send_sem=plane_send, recv_sem=plane_recv,
            device_id={"owner": to + core}, device_id_type=MESH,
        ).start()

    def add_plane(j, value):
        return value + plane_in[j].astype(F32)

    pieces = DirectGather(
        dp_me, 4, at_dp, lambda z: rel_sum.at[core, my_x, my_y, z], piece_send, piece_recv
    )

    def at_x(x):
        return {"owner": (x * ny + my_y) * 2 + core}

    def at_y(y):
        return {"owner": (my_x * ny + y) * 2 + core}

    low_z, high_z = pl.ds(0, 2), pl.ds(2, 2)
    lines = (
        DirectGather(
            my_x, nx, at_x, lambda x: rel_sum.at[core, x, my_y, low_z],
            line_send.at[0], line_recv.at[0],
        ),
        DirectGather(
            my_y, ny, at_y, lambda y: rel_sum.at[core, my_x, y, high_z],
            line_send.at[1], line_recv.at[1],
        ),
    )

    def two(h):
        return pl.ds(2 * h, 2)

    sheets = (
        RingGather(
            my_y, ny, at_y,
            lambda y, h: rel_sum.at[core, two(h) if nx == 4 else slice(None), y,
                                    low_z if nx == 4 else pl.ds(h, 1)],
            sheet_send.at[0], sheet_recv.at[0],
        ),
        RingGather(
            my_x, nx, at_x, lambda x, h: rel_sum.at[core, x, two(h), high_z],
            sheet_send.at[1], sheet_recv.at[1],
        ),
    )

    sent_all(sent, row_send)
    parts = cut_parts(total.shape[0])
    numbers = range(len(parts))

    def back_copy(part, j, q, to):
        low, high = parts[part]
        pltpu.make_async_remote_copy(
            src_ref=sent.at[2 * j + q, pl.ds(low, high - low)],
            dst_ref=received.at[pl.ds(low, high - low), lanes(j * PAIR + core * LANES, LANES)],
            send_sem=back_send.at[part], recv_sem=back_recv.at[part],
            device_id={"owner": to}, device_id_type=MESH,
        ).start()

    def back_own(part, q):
        low, high = parts[part]
        pltpu.make_async_copy(
            sent.at[q, pl.ds(low, high - low)],
            received.at[pl.ds(low, high - low), q * LANES : (q + 1) * LANES],
            back_recv.at[part],
        ).start()

    def push(j):
        sums = lax.dot_general(
            grads[...], one_hot(PAIR, j * PAIR, place), NT, preferred_element_type=F32
        ).astype(BF16)
        for q in range(2):
            sent[2 * j + q] = sums[:, q * LANES : (q + 1) * LANES]
        send_back(0, j)

    def send_back(part, j):
        each_core(
            j, owner_at, functools.partial(back_copy, part), functools.partial(back_own, part)
        )

    def send_later(part):
        for j in range(chips):
            send_back(part, j)

    first, second, third = min(3, chips), min(7, chips), min(10, chips)
    push(0)
    loop(1, first, push)
    indices.finish()
    raw_ring.relay()
    loop(first, second, push)
    raw_ring.finish()
    to_sibling(raw, 0).start()
    to_sibling(relations, 1).start()
    loop(second, third, push)
    loop(third, chips, push)
    send_later(1)
    arrive(raw.at[1 - core], core_recv.at[0])
    arrive(relations.at[1 - core], core_recv.at[1])
    sum_share()
    for j in range(1, chips):
        plane_copy(j)

    rows = total.shape[1]
    share = rows // 4

    def scatter(part, between):
        low, high = parts[part]
        count = rows // tile
        arrive(received.at[low:high], back_recv.at[part])
        for t in range(count):
            for at, act in between:
                if at * count // 8 == t:
                    act()
            cols = slice(t * tile, (t + 1) * tile)
            row = lax.broadcasted_iota(jnp.int32, (received.shape[1], tile), 1) + t * tile
            wanted = jnp.concatenate([asked_column[...]] * (tile // LANES), 1)
            added = jnp.dot(
                received[low:high], jnp.where(wanted == row, 1.0, 0.0).astype(BF16),
                preferred_element_type=F32,
            )
            total[low:high, cols] = added
            shared[low:high, cols] = added.astype(BF16)

    def halves(part):
        return split_part(*parts[part])

    def piece_of(ref, part):
        return lambda z, h: ref.at[pl.ds(*halves(part)[h]), lanes(z * share, share)]

    def dp_sum(part):
        sizes = [halves(part)[h][1] for h in (0, 1, 1, 0, 0, 1)]
        return RingSum(
            dp_me, piece_of(shared, part),
            [dp_in.at[part, i, pl.ds(0, sizes[i])] for i in range(6)],
            dp_send.at[part], dp_recv.at[part],
        )

    sums = [dp_sum(part) for part in numbers]
    alls = [
        RingGather(
            dp_me, 4, at_dp, piece_of(full, part), all_send.at[part], all_recv.at[part]
        )
        for part in numbers
    ]

    def settle(part):
        for h in range(2):
            own = piece_of(total, part)(dp_me, h)
            alls[part].piece(dp_me, h)[...] = (own[...] + sums[part].finish(h)).astype(BF16)
        alls[part].begin()

    def sum_plane():
        mine = share_sum.at[pl.ds(chip * by_piece, by_piece)]
        arrive(plane_in.at[1:], plane_recv)
        rel_sum[core, my_x, my_y, dp_me] = lax.fori_loop(
            1, chips, add_plane, mine[...].astype(F32)
        ).astype(BF16)
        pieces.begin()

    def start_lines():
        pieces.finish()
        for line in lines:
            line.begin()

    def start_sheets():
        for line in lines:
            line.finish()
        for ring in sheets:
            ring.begin()

    def relay_sheets():
        for ring in sheets:
            ring.relay()

    def start_core():
        for ring in sheets:
            ring.finish()
        to_sibling(rel_sum, 2).start()

    scatter(0, [(6, functools.partial(send_later, 2))])
    sums[0].begin()
    sum_plane()
    scatter(1, [(0, start_lines), (2, sums[0].relay)])
    sums[1].begin()
    scatter(2, [
        (0, functools.partial(settle, 0)), (1, start_sheets), (4, sums[1].relay),
        (5, alls[0].relay), (7, relay_sheets),
    ])
    sums[2].begin()
    last = 2

    def lay(c, z):
        for unit in range(share_tiles * per_tile):
            p, i = unit // by_piece, unit % by_piece
            t, r = unit // per_tile, unit % per_tile
            cols = lanes(((c * 4 + z) * share_tiles + t) * LANES, LANES)
            rel_out[16 * r : 16 * r + 16, cols] = rel_sum[c, p // ny, p % ny, z, i]

    settle(1)
    sums[last].relay()
    alls[1].relay()
    settle(last)
    start_core()
    alls[last].relay()
    loop(0, 4, lambda z: lay(core, z))
    arrive(rel_sum.at[1 - core], core_recv.at[2])
    loop(0, 4, lambda z: lay(1 - core, z))

    indices.drain()
    raw_ring.drain()
    to_sibling(raw, 0).wait_send()
    to_sibling(relations, 1).wait_send()
    to_sibling(rel_sum, 2).wait_send()
    pieces.drain()
    for gather in lines + sheets:
        gather.drain()
    for part in numbers:
        sums[part].drain()
    arrive(plane_in.at[1:], plane_send)
    sent_all(asked, ask_send)
    for part, (low, high) in enumerate(parts):
        sent_all(sent.at[:, low:high], back_send.at[part])
    for part in numbers:
        alls[part].finish()
    grad_out[...] = full[...]
    for part in numbers:
        alls[part].drain()


def chunks_of(rows, size):
    return [(start, min(size, rows - start)) for start in range(0, rows, size)]


def adagrad_kernel(
    cuts, table, state, grad, phase, phase_state, rel_grad,
    new_table, new_state, new_phase, new_phase_state,
    table_now, grad_now, phase_now, rel_now, table_in, grad_in, out_sems,
):
    jobs = [
        (table, grad, table_now, grad_now, state, new_table, new_state, start, size)
        for start, size in cuts[0]
    ] + [
        (phase, rel_grad, phase_now, rel_now, phase_state, new_phase, new_phase_state, start, size)
        for start, size in cuts[1]
    ]

    def load(i):
        source, gradient, now, grad_at, _, _, _, start, size = jobs[i]
        cols = pl.ds(start, size)
        return (
            pltpu.make_async_copy(source.at[:, cols], now.at[:, cols], table_in.at[i]),
            pltpu.make_async_copy(gradient.at[:, cols], grad_at.at[:, cols], grad_in.at[i]),
        )

    def store(i):
        _, _, now, _, _, target, _, start, size = jobs[i]
        cols = pl.ds(start, size)
        return pltpu.make_async_copy(now.at[:, cols], target.at[:, cols], out_sems.at[i])

    for i in range(len(jobs)):
        for copy in load(i):
            copy.start()
    for i, (_, _, now, grad_at, old, _, new, start, size) in enumerate(jobs):
        for copy in load(i):
            copy.wait()
        cols = pl.ds(start, size)
        g = grad_at[: now.shape[0], cols].astype(F32)
        fresh = old[cols].reshape(1, size) + jnp.sum(g * g, 0, keepdims=True) * (1.0 / g.shape[0])
        new[cols] = fresh.reshape(size)
        now[:, cols] = now[:, cols] - g * (RATE / jnp.sqrt(fresh))
        store(i).start()
    for i in range(len(jobs)):
        store(i).wait()


def adagrad(table, state, grad, phase, phase_state, rel_grad):
    width, rows = table.shape
    narrow, nrel = phase.shape
    cuts = (chunks_of(rows, 512), chunks_of(nrel, 1024))
    count = len(cuts[0]) + len(cuts[1])
    dma = pltpu.SemaphoreType.DMA
    new_table, new_state, new_phase, new_phase_state = pl.pallas_call(
        functools.partial(adagrad_kernel, cuts),
        out_shape=(
            jax.ShapeDtypeStruct((width, rows), F32),
            jax.ShapeDtypeStruct((rows,), F32),
            jax.ShapeDtypeStruct((narrow, nrel), F32),
            jax.ShapeDtypeStruct((nrel,), F32),
        ),
        in_specs=[HBM, VM, HBM, HBM, VM, HBM],
        out_specs=(HBM, VM, HBM, VM),
        scratch_shapes=[
            pltpu.VMEM((width, rows), F32),
            pltpu.VMEM((width, rows), BF16),
            pltpu.VMEM((narrow, nrel), F32),
            pltpu.VMEM(rel_grad.shape, BF16),
            dma((count,)), dma((count,)), dma((count,)),
        ],
        compiler_params=pltpu.CompilerParams(vmem_limit_bytes=VMEM_LIMIT),
        name="adagrad",
    )(table, state, grad, phase, phase_state, rel_grad)
    return new_table.T, new_state, new_phase.T, new_phase_state


VM = pl.BlockSpec(memory_space=pltpu.VMEM)
HBM = pl.BlockSpec(memory_space=pl.ANY)


def on_device(
    entity_table, entity_state, phase_table, phase_state,
    pull_rows, head_slot, tail_slot, neg_slot, relation,
):
    owners, dps = lax.axis_size("owner"), lax.axis_size("dp")
    table, phase = entity_table.T, phase_table.T
    width, rows = table.shape
    narrow, nrel = phase.shape
    triples = head_slot.shape[1]
    neg = neg_slot.shape[2]
    uses = 2 * triples + neg_slot.shape[1] * neg
    pulls = owners * LANES
    requests = pull_rows.reshape(owners, 1, LANES)
    dma = pltpu.SemaphoreType.DMA
    chips = owners // 2
    padded = -(-narrow // 16) * 16
    share_tiles = -(-(nrel // LANES) // 16) * 2
    piece = -(-(share_tiles * padded // 16) // chips)
    nx, ny = grid_of(owners)
    parts = len(cut_parts(width))
    biggest = max(split_part(*part)[0][1] for part in cut_parts(width))
    grad, rel_total = pl.pallas_call(
        functools.partial(step_kernel, owners, triples // 2, neg),
        out_shape=(
            jax.ShapeDtypeStruct((width, rows), BF16),
            jax.ShapeDtypeStruct((padded, 8 * share_tiles * LANES), BF16),
        ),
        in_specs=[HBM, HBM, VM, VM, VM, VM, VM],
        out_specs=(VM, VM),
        scratch_shapes=[
            pltpu.VMEM((width, rows), F32),
            pltpu.VMEM((narrow, nrel), F32),
            pltpu.VMEM((width, rows), BF16),
            pltpu.VMEM((owners, 1, LANES), jnp.int32),
            pltpu.VMEM((pulls, LANES), jnp.int32),
            pltpu.VMEM((owners, width, LANES), BF16),
            pltpu.VMEM((width, pulls), BF16),
            pltpu.VMEM((width, uses), BF16),
            pltpu.VMEM((width, uses), BF16),
            pltpu.VMEM((width, triples), F32),
            pltpu.VMEM((narrow, triples), F32),
            pltpu.VMEM((narrow, triples), F32),
            pltpu.VMEM((padded, triples), F32),
            pltpu.VMEM((width, pulls), BF16),
            pltpu.VMEM((width, rows), F32),
            pltpu.VMEM((width, rows), BF16),
            pltpu.VMEM((parts, 6, biggest, rows // 4), BF16),
            pltpu.VMEM((width, rows), BF16),
            pltpu.VMEM((2, 4, padded, triples), BF16),
            pltpu.VMEM((2, 4, 1, triples), jnp.int32),
            pltpu.VMEM((chips * piece, 16, LANES), BF16),
            pltpu.VMEM((chips, piece, 16, LANES), BF16),
            pltpu.VMEM((2, nx, ny, 4, piece, 16, LANES), BF16),
            dma((2,)),
            dma, dma, dma, dma((3,)), dma((parts,)), dma((parts,)),
            dma((parts, 6)), dma((parts, 6)), dma((parts, 6)), dma((parts, 6)),
            dma((3,)), dma((3,)), dma((3,)), dma((3,)), dma((6,)), dma((6,)),
            dma, dma, dma((3,)), dma((3,)),
            dma((2, 3)), dma((2, 3)), dma((2, 6)), dma((2, 6)),
        ],
        compiler_params=pltpu.CompilerParams(
            collective_id=0, has_side_effects=True, vmem_limit_bytes=VMEM_LIMIT
        ),
        name="step",
    )(table, phase, requests, head_slot, tail_slot, neg_slot, relation)
    return adagrad(table, entity_state, grad, phase, phase_state, rel_total)


def solution(mesh):
    placed = (
        P("owner", None),
        P("owner"),
        P(),
        P(),
        P(("owner", "dp"), None, None),
        P(("owner", "dp"), None),
        P(("owner", "dp"), None),
        P(("owner", "dp"), None, None),
        P(("owner", "dp"), None),
    )
    return jax.shard_map(
        on_device,
        mesh=mesh,
        in_specs=placed,
        out_specs=(P("owner", None), P("owner"), P(), P()),
        check_vma=False,
    )
```

```python
import functools

import jax
import jax.numpy as jnp
from jax import lax
from jax.experimental import pallas as pl
from jax.experimental.pallas import tpu as pltpu
from jax.sharding import PartitionSpec as P

GAMMA = 2.0
RATE = 0.05
LANES = 128
PAIR = 256
BF16 = jnp.bfloat16
F32 = jnp.float32
MESH = pl.DeviceIdType.MESH
VMEM_LIMIT = 60 * 2**20
NT = (((1,), (1,)), ((), ()))
TN = (((0,), (0,)), ((), ()))


def one_hot(rows, base, index):
    at = lax.broadcasted_iota(jnp.int32, (rows, index.shape[1]), 0) + base
    return jnp.where(at == index, 1.0, 0.0).astype(BF16)


def lanes(start, size):
    return pl.ds(pl.multiple_of(start, LANES), size)


def grid_of(owners):
    chips = owners // 2
    along_y = min(4, chips)
    return chips // along_y, along_y


def partner(me, j, nx, ny, back):
    chip = lax.div(me, 2)
    x, y = lax.div(chip, ny), lax.rem(chip, ny)
    if isinstance(j, int):
        dx = j % nx
        dy = (j // nx + dx) % ny
    else:
        dx = lax.rem(j, nx)
        dy = lax.rem(lax.div(j, nx) + dx, ny)
    x = lax.rem(x + (1 - 2 * back) * dx + back * nx, nx)
    y = lax.rem(y + (1 - 2 * back) * dy + back * ny, ny)
    return (x * ny + y) * 2


def positions(slots, me, nx, ny):
    chip = slots >> 8
    way = 1 - 2 * ((slots >> 7) & 1)
    x, y = chip // ny, chip & (ny - 1)
    mine = me // 2
    dx = (way * (mine // ny - x)) & (nx - 1)
    dy = (way * (mine % ny - y)) & (ny - 1)
    j = ((dy - dx) & (ny - 1)) * nx + dx
    return j * PAIR + (slots & (PAIR - 1))


def as_column(row):
    return jnp.broadcast_to(row, (LANES, row.shape[1])).T[:, :1]


def as_row(column):
    return jnp.broadcast_to(column, (column.shape[0], LANES)).T[:1, :]


def greet(me, owners, dp_me, dps):
    barrier = pltpu.get_barrier_semaphore()

    def hello(k, _):
        pl.semaphore_signal(
            barrier, inc=1, device_id={"owner": (me + k) % owners}, device_id_type=MESH
        )
        return 0

    lax.fori_loop(1, owners, hello, 0)
    for k in range(1, dps):
        pl.semaphore_signal(
            barrier, inc=1, device_id={"dp": (dp_me + k) % dps}, device_id_type=MESH
        )
    pl.semaphore_wait(barrier, owners - 1 + dps - 1)


def block_grads(b, group, neg, used, cosine, sine, grads, phase_grads):
    triples = 2 * group
    cols = lanes(b * group, group)
    tail_cols = lanes(triples + b * group, group)
    neg_cols = lanes(2 * triples + b * neg, neg)
    cos, sin = cosine[:, cols], sine[:, cols]
    width = cos.shape[0]
    heads = used[:, cols].astype(F32)
    head_re, head_im = heads[:width], heads[width:]
    rot_re = head_re * cos - head_im * sin
    rot_im = head_re * sin + head_im * cos
    rotated = jnp.concatenate([rot_re, rot_im], 0)
    diff = rotated - used[:, tail_cols].astype(F32)
    pos_score = GAMMA - jnp.sum(diff * diff, 0, keepdims=True)
    rot_half = rotated.astype(BF16)
    rot_wide = rot_half.astype(F32)
    negs = used[:, neg_cols]
    neg_wide = negs.astype(F32)
    row_norm = as_column(jnp.sum(rot_wide * rot_wide, 0, keepdims=True))
    neg_norm = jnp.sum(neg_wide * neg_wide, 0, keepdims=True)
    cross = lax.dot_general(rot_half, negs, TN, preferred_element_type=F32)
    neg_score = GAMMA - (row_norm + neg_norm - 2.0 * cross)
    weight = jax.nn.sigmoid(neg_score) * (1.0 / neg)
    weight_half = weight.astype(BF16)
    diff_grad = (2.0 * jax.nn.sigmoid(-pos_score)) * diff
    row_sum = as_row(jnp.sum(weight, 1, keepdims=True))
    col_sum = jnp.sum(weight, 0, keepdims=True)
    rot_grad = (
        diff_grad
        - (2.0 * row_sum) * rot_wide
        + 2.0 * lax.dot_general(negs, weight_half, NT, preferred_element_type=F32)
    )
    grads[:, neg_cols] = (
        2.0 * jnp.dot(rot_half, weight_half, preferred_element_type=F32)
        - (2.0 * col_sum) * neg_wide
    ).astype(BF16)
    grads[:, tail_cols] = (-diff_grad).astype(BF16)
    grad_re, grad_im = rot_grad[:width], rot_grad[width:]
    phase_grads[:width, cols] = grad_im * rot_re - grad_re * rot_im
    grads[:, cols] = jnp.concatenate(
        [grad_re * cos + grad_im * sin, grad_im * cos - grad_re * sin], 0
    ).astype(BF16)


def arrive(ref, sem):
    pltpu.make_async_copy(ref, ref, sem).wait()


class RingSum:
    def __init__(self, dp_me, piece, landing, send, recv):
        self.piece, self.landing, self.send, self.recv = piece, landing, send, recv
        self.me, self.right, self.left = dp_me, (dp_me + 1) % 4, (dp_me + 3) % 4
        self.opposite = (dp_me + 2) % 4

    def copy(self, src, slot, to):
        return pltpu.make_async_remote_copy(
            src_ref=src, dst_ref=self.landing[slot],
            send_sem=self.send.at[slot], recv_sem=self.recv.at[slot],
            device_id={"dp": to}, device_id_type=MESH,
        )

    def part(self, slot):
        z, h, to = (
            (self.opposite, 0, self.right),
            (self.opposite, 1, self.left),
            (self.right, 1, self.right),
            (self.left, 0, self.left),
            (self.right, 0, self.right),
            (self.left, 1, self.left),
        )[slot]
        return self.copy(self.piece(z, h), slot, to)

    def begin(self):
        for slot in range(4):
            self.part(slot).start()

    def relay(self):
        for slot, z, h in ((0, self.right, 0), (1, self.left, 1)):
            arrive(self.landing[slot], self.recv.at[slot])
            spot = self.piece(z, h)
            spot[...] = (spot[...].astype(F32) + self.landing[slot][...].astype(F32)).astype(BF16)
            self.part(4 + slot).start()

    def finish(self, h):
        slots = (4, 3) if h == 0 else (5, 2)
        for slot in slots:
            arrive(self.landing[slot], self.recv.at[slot])
        return self.landing[slots[0]][...].astype(F32) + self.landing[slots[1]][...].astype(F32)

    def drain(self):
        for slot in range(6):
            self.part(slot).wait_send()


class RingGather:
    def __init__(self, me, count, device, piece, send, recv):
        self.device, self.piece, self.send, self.recv = device, piece, send, recv
        self.count = count
        self.me, self.right, self.left = me, (me + 1) % count, (me + count - 1) % count
        self.opposite = (me + 2) % count

    def part(self, slot):
        z, h, to = (
            (self.me, 0, self.right),
            (self.me, 1, self.left),
            (self.me, 1, self.right),
            (self.me, 0, self.left),
            (self.left, 0, self.right),
            (self.right, 1, self.left),
        )[slot]
        return pltpu.make_async_remote_copy(
            src_ref=self.piece(z, h), dst_ref=self.piece(z, h),
            send_sem=self.send.at[slot], recv_sem=self.recv.at[slot],
            device_id=self.device(to), device_id_type=MESH,
        )

    def begin(self):
        if self.count == 4:
            for slot in range(4):
                self.part(slot).start()

    def relay(self):
        if self.count == 4:
            arrive(self.piece(self.left, 0), self.recv.at[0])
            self.part(4).start()
            arrive(self.piece(self.right, 1), self.recv.at[1])
            self.part(5).start()

    def finish(self):
        if self.count == 4:
            arrive(self.piece(self.left, 1), self.recv.at[2])
            arrive(self.piece(self.right, 0), self.recv.at[3])
            arrive(self.piece(self.opposite, 0), self.recv.at[4])
            arrive(self.piece(self.opposite, 1), self.recv.at[5])

    def drain(self):
        if self.count == 4:
            for slot in range(6):
                self.part(slot).wait_send()


class DirectGather:
    def __init__(self, me, count, device, piece, send, recv):
        self.me, self.count, self.device, self.piece = me, count, device, piece
        self.send, self.recv = send, recv

    def part(self, k):
        return pltpu.make_async_remote_copy(
            src_ref=self.piece(self.me), dst_ref=self.piece(self.me),
            send_sem=self.send.at[k - 1], recv_sem=self.recv.at[k - 1],
            device_id=self.device((self.me + k) % self.count), device_id_type=MESH,
        )

    def begin(self):
        for k in range(1, self.count):
            self.part(k).start()

    def finish(self):
        for k in range(1, self.count):
            source = (self.me + self.count - k) % self.count
            arrive(self.piece(source), self.recv.at[k - 1])

    def drain(self):
        for k in range(1, self.count):
            self.part(k).wait_send()


def cut_parts(features):
    units = features // 16
    counts = (10, 9, 6) if units == 25 else (units - 4, 2, 2)
    bounds = [0]
    for count in counts:
        bounds.append(bounds[-1] + 16 * count)
    return tuple(zip(bounds[:-1], bounds[1:]))


def split_part(low, high):
    cut = low + -(-(high - low) // 32) * 16
    return ((low, cut - low), (cut, high - cut))


def step_kernel(
    owners, group, neg,
    table_hbm, phase_hbm, requests, head_slot, tail_slot, neg_slot, relation,
    grad_out, rel_out,
    table, phase, table_half, asked, asked_column, sent, pulled, used, grads,
    theta, cosine, sine, phase_grads,
    received, total, shared, dp_in, full,
    raw, relations, share_sum, plane_in, rel_sum,
    load_sems, ask_send, ask_recv, row_send, row_recv, back_send, back_recv,
    dp_send, dp_recv, all_send, all_recv,
    core_send, core_recv, index_send, index_recv, raw_send, raw_recv,
    plane_send, plane_recv, piece_send, piece_recv,
    line_send, line_recv, sheet_send, sheet_recv,
):
    nx, ny = grid_of(owners)
    chips = nx * ny
    me = lax.axis_index("owner")
    dp_me = lax.axis_index("dp")
    core = me % 2
    load_table = pltpu.make_async_copy(table_hbm, table, load_sems.at[0])
    load_phase = pltpu.make_async_copy(phase_hbm, phase, load_sems.at[1])
    load_table.start()
    load_phase.start()
    greet(me, owners, dp_me, 4)

    def owner_at(j, q):
        return partner(me, j, nx, ny, 1 - q) + q

    def worker_at(j, q):
        return partner(me, j, nx, ny, core) + q

    def each_core(j, place_of, start, start_own):
        for q in range(2):
            to = place_of(j, q)
            if isinstance(j, int) and j == 0:
                pl.when(to != me)(functools.partial(start, j, q, to))
                pl.when(to == me)(functools.partial(start_own, q))
            else:
                start(j, q, to)

    def sent_all(ref, sem):
        arrive(ref.at[pl.ds(0, owners - 1)], sem)

    def loop(low, high, act):
        def body(j, _):
            act(j)
            return 0

        lax.fori_loop(low, high, body, 0)

    def ask(j, q, to):
        pltpu.make_async_remote_copy(
            src_ref=requests.at[to], dst_ref=asked.at[2 * j + core],
            send_sem=ask_send, recv_sem=ask_recv,
            device_id={"owner": to}, device_id_type=MESH,
        ).start()

    def ask_own(q):
        pltpu.make_async_copy(requests.at[me], asked.at[q], ask_recv).start()

    for j in range(chips):
        each_core(j, owner_at, ask, ask_own)

    def at_dp(z):
        return {"dp": z}

    relations[core, dp_me] = relation[...]
    indices = DirectGather(
        dp_me, 4, at_dp, lambda z: relations.at[core, z], index_send, index_recv
    )
    indices.begin()
    load_table.wait()
    table_half[...] = table[...].astype(BF16)

    cuts = (0, chips // 2, chips - chips // 4, chips - chips // 8, chips)

    def row_copy(cut, j, q, to):
        pltpu.make_async_remote_copy(
            src_ref=sent.at[2 * j + q],
            dst_ref=pulled.at[:, lanes(j * PAIR + core * LANES, LANES)],
            send_sem=row_send, recv_sem=row_recv.at[cut],
            device_id={"owner": to}, device_id_type=MESH,
        ).start()

    def row_own(q):
        pltpu.make_async_copy(
            sent.at[q], pulled.at[:, q * LANES : (q + 1) * LANES], row_recv.at[0]
        ).start()

    def fetch(cut, j):
        wanted = jnp.concatenate([asked[2 * j], asked[2 * j + 1]], 1)
        asked_column[pl.ds(pl.multiple_of(j * PAIR, PAIR), PAIR)] = jnp.broadcast_to(
            wanted, (LANES, PAIR)
        ).T
        rows = jnp.dot(
            table_half[...], one_hot(table_half.shape[1], 0, wanted), preferred_element_type=F32
        ).astype(BF16)
        for q in range(2):
            sent[2 * j + q] = rows[:, q * LANES : (q + 1) * LANES]
        each_core(j, worker_at, functools.partial(row_copy, cut), row_own)

    arrive(asked, ask_recv)
    fetch(0, 0)
    for cut in range(4):
        loop(max(1, cuts[cut]), cuts[cut + 1], functools.partial(fetch, cut))

    load_phase.wait()
    rel_index = relation[...]
    nrel = phase.shape[1]
    width = phase.shape[0]
    step = 1024
    whole = nrel // step

    def phase_part(start, size):
        part = phase[:, lanes(start, size)]
        high = part.astype(BF16).astype(F32)
        both = jnp.concatenate([high, part - high], 0).astype(BF16)
        return jnp.dot(both, one_hot(size, start, rel_index), preferred_element_type=F32)

    theta[...] = jnp.zeros_like(theta)

    def add_phase(k, _):
        theta[...] += phase_part(k * step, step)
        return 0

    lax.fori_loop(0, whole, add_phase, 0)
    if nrel % step:
        theta[...] += phase_part(whole * step, nrel % step)
    angle = theta[:width] + theta[width:]
    cosine[...] = jnp.cos(angle)
    sine[...] = jnp.sin(angle)

    slots = [head_slot[...], tail_slot[...]]
    slots += [neg_slot[0, b : b + 1] for b in range(neg_slot.shape[1])]
    place = positions(jnp.concatenate(slots, 1), me, nx, ny)
    uses = place.shape[1]
    tile = 256
    for cut in range(4):
        low, high = cuts[cut], cuts[cut + 1]
        if low == high:
            continue
        arrive(pulled.at[:, low * PAIR : high * PAIR], row_recv.at[cut])
        for t in range(uses // tile):
            cols = slice(t * tile, (t + 1) * tile)
            found = jnp.dot(
                pulled[:, low * PAIR : high * PAIR],
                one_hot((high - low) * PAIR, low * PAIR, place[:, cols]),
                preferred_element_type=F32,
            ).astype(BF16)
            used[:, cols] = found if low == 0 else used[:, cols] + found

    phase_grads[width:] = jnp.zeros_like(phase_grads[width:])
    for b in range(2):
        block_grads(b, group, neg, used, cosine, sine, grads, phase_grads)

    raw[core, dp_me] = phase_grads[...].astype(BF16)
    padded = raw.shape[2]
    raw_halves = split_part(0, padded)
    raw_ring = RingGather(
        dp_me, 4, at_dp, lambda z, h: raw.at[core, z, pl.ds(*raw_halves[h])],
        raw_send, raw_recv,
    )
    raw_ring.begin()
    sibling = me + 1 - 2 * core

    def to_sibling(ref, slot):
        return pltpu.make_async_remote_copy(
            src_ref=ref.at[core], dst_ref=ref.at[core],
            send_sem=core_send.at[slot], recv_sem=core_recv.at[slot],
            device_id={"owner": sibling}, device_id_type=MESH,
        )

    per_tile = padded // 16
    share_tiles = -(-(nrel // LANES) // 16) * 2
    by_piece = rel_sum.shape[4]
    chip = me // 2
    my_x, my_y = chip // ny, chip % ny
    eighth = core * 4 + dp_me

    def sum_share():
        base = eighth * share_tiles * LANES
        for t in range(share_tiles // 2):
            found = None
            for c in range(2):
                for z in range(4):
                    part = lax.dot_general(
                        raw[c, z], one_hot(PAIR, base + t * PAIR, relations[c, z]), NT,
                        preferred_element_type=F32,
                    )
                    found = part if found is None else found + part
            found = found.astype(BF16)
            for i in range(2):
                at = (2 * t + i) * per_tile
                share_sum[at : at + per_tile] = found[
                    :, i * LANES : (i + 1) * LANES
                ].reshape(per_tile, 16, LANES)
        filled = share_tiles * per_tile
        if filled < share_sum.shape[0]:
            share_sum[filled:] = jnp.zeros_like(share_sum[filled:])

    def plane_copy(j):
        to = partner(me, j, nx, ny, core)
        pltpu.make_async_remote_copy(
            src_ref=share_sum.at[pl.ds(lax.div(to, 2) * by_piece, by_piece)],
            dst_ref=plane_in.at[j], send_sem=plane_send, recv_sem=plane_recv,
            device_id={"owner": to + core}, device_id_type=MESH,
        ).start()

    def add_plane(j, value):
        return value + plane_in[j].astype(F32)

    pieces = DirectGather(
        dp_me, 4, at_dp, lambda z: rel_sum.at[core, my_x, my_y, z], piece_send, piece_recv
    )

    def at_x(x):
        return {"owner": (x * ny + my_y) * 2 + core}

    def at_y(y):
        return {"owner": (my_x * ny + y) * 2 + core}

    low_z, high_z = pl.ds(0, 2), pl.ds(2, 2)
    lines = (
        DirectGather(
            my_x, nx, at_x, lambda x: rel_sum.at[core, x, my_y, low_z],
            line_send.at[0], line_recv.at[0],
        ),
        DirectGather(
            my_y, ny, at_y, lambda y: rel_sum.at[core, my_x, y, high_z],
            line_send.at[1], line_recv.at[1],
        ),
    )

    def two(h):
        return pl.ds(2 * h, 2)

    sheets = (
        RingGather(
            my_y, ny, at_y,
            lambda y, h: rel_sum.at[core, two(h) if nx == 4 else slice(None), y,
                                    low_z if nx == 4 else pl.ds(h, 1)],
            sheet_send.at[0], sheet_recv.at[0],
        ),
        RingGather(
            my_x, nx, at_x, lambda x, h: rel_sum.at[core, x, two(h), high_z],
            sheet_send.at[1], sheet_recv.at[1],
        ),
    )

    sent_all(sent, row_send)
    parts = cut_parts(total.shape[0])
    numbers = range(len(parts))

    def back_copy(part, j, q, to):
        low, high = parts[part]
        pltpu.make_async_remote_copy(
            src_ref=sent.at[2 * j + q, pl.ds(low, high - low)],
            dst_ref=received.at[pl.ds(low, high - low), lanes(j * PAIR + core * LANES, LANES)],
            send_sem=back_send.at[part], recv_sem=back_recv.at[part],
            device_id={"owner": to}, device_id_type=MESH,
        ).start()

    def back_own(part, q):
        low, high = parts[part]
        pltpu.make_async_copy(
            sent.at[q, pl.ds(low, high - low)],
            received.at[pl.ds(low, high - low), q * LANES : (q + 1) * LANES],
            back_recv.at[part],
        ).start()

    def push(j):
        sums = lax.dot_general(
            grads[...], one_hot(PAIR, j * PAIR, place), NT, preferred_element_type=F32
        ).astype(BF16)
        for q in range(2):
            sent[2 * j + q] = sums[:, q * LANES : (q + 1) * LANES]
        send_back(0, j)

    def send_back(part, j):
        each_core(
            j, owner_at, functools.partial(back_copy, part), functools.partial(back_own, part)
        )

    def send_later(part):
        for j in range(chips):
            send_back(part, j)

    first, second, third = min(3, chips), min(7, chips), min(10, chips)
    push(0)
    loop(1, first, push)
    indices.finish()
    raw_ring.relay()
    loop(first, second, push)
    raw_ring.finish()
    to_sibling(raw, 0).start()
    to_sibling(relations, 1).start()
    loop(second, third, push)
    loop(third, chips, push)
    send_later(1)
    arrive(raw.at[1 - core], core_recv.at[0])
    arrive(relations.at[1 - core], core_recv.at[1])
    sum_share()
    for j in range(1, chips):
        plane_copy(j)

    rows = total.shape[1]
    share = rows // 4

    def scatter(part, between):
        low, high = parts[part]
        count = rows // tile
        arrive(received.at[low:high], back_recv.at[part])
        for t in range(count):
            for at, act in between:
                if at * count // 8 == t:
                    act()
            cols = slice(t * tile, (t + 1) * tile)
            row = lax.broadcasted_iota(jnp.int32, (received.shape[1], tile), 1) + t * tile
            wanted = jnp.concatenate([asked_column[...]] * (tile // LANES), 1)
            added = jnp.dot(
                received[low:high], jnp.where(wanted == row, 1.0, 0.0).astype(BF16),
                preferred_element_type=F32,
            )
            total[low:high, cols] = added
            shared[low:high, cols] = added.astype(BF16)

    def halves(part):
        return split_part(*parts[part])

    def piece_of(ref, part):
        return lambda z, h: ref.at[pl.ds(*halves(part)[h]), lanes(z * share, share)]

    def dp_sum(part):
        sizes = [halves(part)[h][1] for h in (0, 1, 1, 0, 0, 1)]
        return RingSum(
            dp_me, piece_of(shared, part),
            [dp_in.at[part, i, pl.ds(0, sizes[i])] for i in range(6)],
            dp_send.at[part], dp_recv.at[part],
        )

    sums = [dp_sum(part) for part in numbers]
    alls = [
        RingGather(
            dp_me, 4, at_dp, piece_of(full, part), all_send.at[part], all_recv.at[part]
        )
        for part in numbers
    ]

    def settle(part):
        for h in range(2):
            own = piece_of(total, part)(dp_me, h)
            alls[part].piece(dp_me, h)[...] = (own[...] + sums[part].finish(h)).astype(BF16)
        alls[part].begin()

    def sum_plane():
        mine = share_sum.at[pl.ds(chip * by_piece, by_piece)]
        arrive(plane_in.at[1:], plane_recv)
        rel_sum[core, my_x, my_y, dp_me] = lax.fori_loop(
            1, chips, add_plane, mine[...].astype(F32)
        ).astype(BF16)
        pieces.begin()

    def start_lines():
        pieces.finish()
        for line in lines:
            line.begin()

    def start_sheets():
        for line in lines:
            line.finish()
        for ring in sheets:
            ring.begin()

    def relay_sheets():
        for ring in sheets:
            ring.relay()

    def start_core():
        for ring in sheets:
            ring.finish()
        to_sibling(rel_sum, 2).start()

    scatter(0, [(6, functools.partial(send_later, 2))])
    sums[0].begin()
    sum_plane()
    scatter(1, [(0, start_lines), (2, sums[0].relay)])
    sums[1].begin()
    scatter(2, [
        (0, functools.partial(settle, 0)), (1, start_sheets), (4, sums[1].relay),
        (5, alls[0].relay), (7, relay_sheets),
    ])
    sums[2].begin()
    last = 2

    def lay(c, z):
        for unit in range(share_tiles * per_tile):
            p, i = unit // by_piece, unit % by_piece
            t, r = unit // per_tile, unit % per_tile
            cols = lanes(((c * 4 + z) * share_tiles + t) * LANES, LANES)
            rel_out[16 * r : 16 * r + 16, cols] = rel_sum[c, p // ny, p % ny, z, i]

    settle(1)
    sums[last].relay()
    alls[1].relay()
    settle(last)
    start_core()
    alls[last].relay()
    loop(0, 4, lambda z: lay(core, z))
    arrive(rel_sum.at[1 - core], core_recv.at[2])
    loop(0, 4, lambda z: lay(1 - core, z))

    indices.drain()
    raw_ring.drain()
    to_sibling(raw, 0).wait_send()
    to_sibling(relations, 1).wait_send()
    to_sibling(rel_sum, 2).wait_send()
    pieces.drain()
    for gather in lines + sheets:
        gather.drain()
    for part in numbers:
        sums[part].drain()
    arrive(plane_in.at[1:], plane_send)
    sent_all(asked, ask_send)
    for part, (low, high) in enumerate(parts):
        sent_all(sent.at[:, low:high], back_send.at[part])
    for part in numbers:
        alls[part].finish()
    grad_out[...] = full[...]
    for part in numbers:
        alls[part].drain()


def chunks_of(rows, size):
    return [(start, min(size, rows - start)) for start in range(0, rows, size)]


def adagrad_kernel(
    cuts, table, state, grad, phase, phase_state, rel_grad,
    new_table, new_state, new_phase, new_phase_state,
    table_now, grad_now, phase_now, rel_now, table_in, grad_in, out_sems,
):
    jobs = [
        (table, grad, table_now, grad_now, state, new_table, new_state, start, size)
        for start, size in cuts[0]
    ] + [
        (phase, rel_grad, phase_now, rel_now, phase_state, new_phase, new_phase_state, start, size)
        for start, size in cuts[1]
    ]

    def load(i):
        source, gradient, now, grad_at, _, _, _, start, size = jobs[i]
        cols = pl.ds(start, size)
        return (
            pltpu.make_async_copy(source.at[:, cols], now.at[:, cols], table_in.at[i]),
            pltpu.make_async_copy(gradient.at[:, cols], grad_at.at[:, cols], grad_in.at[i]),
        )

    def store(i):
        _, _, now, _, _, target, _, start, size = jobs[i]
        cols = pl.ds(start, size)
        return pltpu.make_async_copy(now.at[:, cols], target.at[:, cols], out_sems.at[i])

    for i in range(len(jobs)):
        for copy in load(i):
            copy.start()
    for i, (_, _, now, grad_at, old, _, new, start, size) in enumerate(jobs):
        for copy in load(i):
            copy.wait()
        cols = pl.ds(start, size)
        g = grad_at[: now.shape[0], cols].astype(F32)
        fresh = old[cols].reshape(1, size) + jnp.sum(g * g, 0, keepdims=True) * (1.0 / g.shape[0])
        new[cols] = fresh.reshape(size)
        now[:, cols] = now[:, cols] - g * (RATE / jnp.sqrt(fresh))
        store(i).start()
    for i in range(len(jobs)):
        store(i).wait()


def adagrad(table, state, grad, phase, phase_state, rel_grad):
    width, rows = table.shape
    narrow, nrel = phase.shape
    cuts = (chunks_of(rows, 512), chunks_of(nrel, 1024))
    count = len(cuts[0]) + len(cuts[1])
    dma = pltpu.SemaphoreType.DMA
    new_table, new_state, new_phase, new_phase_state = pl.pallas_call(
        functools.partial(adagrad_kernel, cuts),
        out_shape=(
            jax.ShapeDtypeStruct((width, rows), F32),
            jax.ShapeDtypeStruct((rows,), F32),
            jax.ShapeDtypeStruct((narrow, nrel), F32),
            jax.ShapeDtypeStruct((nrel,), F32),
        ),
        in_specs=[HBM, VM, HBM, HBM, VM, HBM],
        out_specs=(HBM, VM, HBM, VM),
        scratch_shapes=[
            pltpu.VMEM((width, rows), F32),
            pltpu.VMEM((width, rows), BF16),
            pltpu.VMEM((narrow, nrel), F32),
            pltpu.VMEM(rel_grad.shape, BF16),
            dma((count,)), dma((count,)), dma((count,)),
        ],
        compiler_params=pltpu.CompilerParams(vmem_limit_bytes=VMEM_LIMIT),
        name="adagrad",
    )(table, state, grad, phase, phase_state, rel_grad)
    return new_table.T, new_state, new_phase.T, new_phase_state


VM = pl.BlockSpec(memory_space=pltpu.VMEM)
HBM = pl.BlockSpec(memory_space=pl.ANY)


def on_device(
    entity_table, entity_state, phase_table, phase_state,
    pull_rows, head_slot, tail_slot, neg_slot, relation,
):
    owners, dps = lax.axis_size("owner"), lax.axis_size("dp")
    table, phase = entity_table.T, phase_table.T
    width, rows = table.shape
    narrow, nrel = phase.shape
    triples = head_slot.shape[1]
    neg = neg_slot.shape[2]
    uses = 2 * triples + neg_slot.shape[1] * neg
    pulls = owners * LANES
    requests = pull_rows.reshape(owners, 1, LANES)
    dma = pltpu.SemaphoreType.DMA
    chips = owners // 2
    padded = -(-narrow // 16) * 16
    share_tiles = -(-(nrel // LANES) // 16) * 2
    piece = -(-(share_tiles * padded // 16) // chips)
    nx, ny = grid_of(owners)
    parts = len(cut_parts(width))
    biggest = max(split_part(*part)[0][1] for part in cut_parts(width))
    grad, rel_total = pl.pallas_call(
        functools.partial(step_kernel, owners, triples // 2, neg),
        out_shape=(
            jax.ShapeDtypeStruct((width, rows), BF16),
            jax.ShapeDtypeStruct((padded, 8 * share_tiles * LANES), BF16),
        ),
        in_specs=[HBM, HBM, VM, VM, VM, VM, VM],
        out_specs=(VM, VM),
        scratch_shapes=[
            pltpu.VMEM((width, rows), F32),
            pltpu.VMEM((narrow, nrel), F32),
            pltpu.VMEM((width, rows), BF16),
            pltpu.VMEM((owners, 1, LANES), jnp.int32),
            pltpu.VMEM((pulls, LANES), jnp.int32),
            pltpu.VMEM((owners, width, LANES), BF16),
            pltpu.VMEM((width, pulls), BF16),
            pltpu.VMEM((width, uses), BF16),
            pltpu.VMEM((width, uses), BF16),
            pltpu.VMEM((width, triples), F32),
            pltpu.VMEM((narrow, triples), F32),
            pltpu.VMEM((narrow, triples), F32),
            pltpu.VMEM((padded, triples), F32),
            pltpu.VMEM((width, pulls), BF16),
            pltpu.VMEM((width, rows), F32),
            pltpu.VMEM((width, rows), BF16),
            pltpu.VMEM((parts, 6, biggest, rows // 4), BF16),
            pltpu.VMEM((width, rows), BF16),
            pltpu.VMEM((2, 4, padded, triples), BF16),
            pltpu.VMEM((2, 4, 1, triples), jnp.int32),
            pltpu.VMEM((chips * piece, 16, LANES), BF16),
            pltpu.VMEM((chips, piece, 16, LANES), BF16),
            pltpu.VMEM((2, nx, ny, 4, piece, 16, LANES), BF16),
            dma((2,)),
            dma, dma, dma, dma((4,)), dma((parts,)), dma((parts,)),
            dma((parts, 6)), dma((parts, 6)), dma((parts, 6)), dma((parts, 6)),
            dma((3,)), dma((3,)), dma((3,)), dma((3,)), dma((6,)), dma((6,)),
            dma, dma, dma((3,)), dma((3,)),
            dma((2, 3)), dma((2, 3)), dma((2, 6)), dma((2, 6)),
        ],
        compiler_params=pltpu.CompilerParams(
            collective_id=0, has_side_effects=True, vmem_limit_bytes=VMEM_LIMIT
        ),
        name="step",
    )(table, phase, requests, head_slot, tail_slot, neg_slot, relation)
    return adagrad(table, entity_state, grad, phase, phase_state, rel_total)


def solution(mesh):
    placed = (
        P("owner", None),
        P("owner"),
        P(),
        P(),
        P(("owner", "dp"), None, None),
        P(("owner", "dp"), None),
        P(("owner", "dp"), None),
        P(("owner", "dp"), None, None),
        P(("owner", "dp"), None),
    )
    return jax.shard_map(
        on_device,
        mesh=mesh,
        in_specs=placed,
        out_specs=(P("owner", None), P("owner"), P(), P()),
        check_vma=False,
    )
```
